512 devices in a mesh: dp: 16 (over y_hi, x, core), mp: 32 (over z, y_lo).
Axes of the slice: x: 4, y: 4 (y_hi: 2, y_lo: 2; y = y_hi * 2 + y_lo), z: 16, core: 2. Of those that a mesh axis runs over, the one named last changes fastest.
Arguments:
- hidden: bfloat16 [32768, 5120], P('dp', 'mp'), may hold values from -6 to 6
- mod_table: bfloat16 [50, 2, 5120], P(None, None, 'mp'), may hold values from -3 to 3
- timestep: int32 [16], P('dp'), may hold values from 0 to 49
- head_weight: bfloat16 [5120, 64], P('mp'), may hold values from -0.078125 to 0.078125
- conv_in: bfloat16 [16, 27, 384], replicated, may hold values from -0.3125 to 0.3125
- conv_mid: bfloat16 [384, 27, 384], P('dp'), may hold values from -0.0625 to 0.0625
- patch_weight: bfloat16 [384, 1024], replicated, may hold values from -0.3125 to 0.3125
- text_emb: float32 [16, 1024], P('dp'), may hold values from -6 to 6
Outputs:
- reward: float32 [16], P('dp')
- head_grad: float32 [5120, 64], P('mp')
- hidden_grad: bfloat16 [32768, 5120], P('dp', 'mp')
The draws below stay inside these ranges and needn't reach their ends.
Inputs may be any that keep to these rules, and one draw needn't show every extreme that they name: One timestep index a video.
All inputs are finite; a program needn't handle non-finite values.
Results may differ from the reference program's by a relative error of at most 0.029.
Values may be sent and summed in bfloat16 or wider, within the bound.
A program may use at most 64 MiB of HBM per device.

```python
import jax
import jax.numpy as jnp
from jax import lax

D = 5120
C = 16
CH = 384
EMB = 1024
NSTEPS = 50
LW = 64
LT = 2
LH = 64
VIDEOS = 16
S = 2048
TOKENS = 32768


def with_ends(array, rng, smallest, largest):
    longest = array.shape.index(max(array.shape))
    spots = []
    for shift in (0, 1):
        where = [jax.random.randint(jax.random.fold_in(rng, axis), (), 0, length) for axis, length in enumerate(array.shape)]
        where[longest] = (where[longest] + shift) % array.shape[longest]
        spots.append(tuple(where))
    return array.at[spots[0]].set(smallest).at[spots[1]].set(largest)


def steps_of(rng, shape, split, smallest, high):
    def one(position, blocks):
        steps = jax.random.uniform(jax.random.fold_in(jax.random.fold_in(rng, 6), position), (blocks,), jnp.float32, smallest / len(split), high / len(split))
        return jnp.repeat(jnp.exp(steps), shape[position] // blocks).reshape((-1,) + (1,) * (len(shape) - position - 1))

    level = one(*split[0])
    for cut in split[1:]:
        level = level * one(*cut)
    return level


def bell_draw(rng, dims, spread, most, split=(), kind=jnp.bfloat16):
    level = steps_of(rng, dims, split, -0.22, 0.18) if split else 1.0
    array = jax.random.normal(rng, dims, jnp.float32) * spread * level
    return jnp.minimum(jnp.maximum(array, -most), most).astype(kind)


def setup_inputs(seed: int = 0) -> dict:
    arg_keys = jax.random.split(jax.random.key(seed), 9)
    return {
        "hidden": bell_draw(arg_keys[0], (TOKENS, D), 1.0, 6.0, ((0, 16), (1, 32))),
        "mod_table": bell_draw(arg_keys[1], (NSTEPS, 2, D), 0.5, 3.0, ((2, 32),)),
        "timestep": with_ends(jax.random.randint(arg_keys[2], (VIDEOS,), 0, NSTEPS), jax.random.fold_in(arg_keys[2], 1), 0, NSTEPS - 1).astype(jnp.int32),
        "head_weight": bell_draw(arg_keys[3], (D, 4 * C), D ** -0.5, 0.078125, ((0, 32),)),
        "conv_in": bell_draw(arg_keys[4], (C, 27, CH), (27 * C) ** -0.5, 0.3125),
        "conv_mid": bell_draw(arg_keys[5], (CH, 27, CH), (27 * CH) ** -0.5, 0.0625, ((0, 16),)),
        "patch_weight": bell_draw(arg_keys[6], (CH, EMB), CH ** -0.5, 0.3125),
        "text_emb": bell_draw(arg_keys[7], (VIDEOS, EMB), 1.0, 6.0, ((0, 16),), jnp.float32),
    }


def silu_slope(value):
    gate = jax.nn.sigmoid(value)
    return gate * (1.0 + value * (1.0 - gate))

def scoring(pooled, video_text, patch_weight):
    embedded = jnp.dot(pooled, patch_weight.astype(jnp.float32), precision=lax.Precision.HIGHEST)
    embed_length = jnp.sqrt(lax.optimization_barrier(jnp.sum(embedded * embedded, axis=1)) + 1e-06)
    text_length = jnp.sqrt(jnp.sum(video_text * video_text) + 1e-06)
    cosine = jnp.dot(embedded, video_text, precision=lax.Precision.HIGHEST) / (embed_length * text_length)
    return 100.0 * jnp.mean(cosine)

def conv_apply(field, weight, reverse_time):
    time_pad = (0, 2) if reverse_time else (2, 0)
    padded = jnp.pad(field, (time_pad, (1, 1), (1, 1), (0, 0)))
    frames, rows, cols = (field.shape[0], field.shape[1], field.shape[2])
    width_out = weight.shape[0] if reverse_time else weight.shape[2]
    summed = jnp.zeros((frames, rows, cols, width_out), jnp.float32)
    for tap_index in range(27):
        step_time, step_rows, step_cols = (tap_index // 9, tap_index // 3 % 3, tap_index % 3)
        view = padded[step_time:step_time + frames, step_rows:step_rows + rows, step_cols:step_cols + cols].astype(jnp.float32)
        if reverse_time:
            summed = summed + jnp.einsum('thwo,io->thwi', view, weight[:, 26 - tap_index, :].astype(jnp.float32), precision=lax.Precision.HIGHEST)
        else:
            summed = summed + jnp.einsum('thwi,io->thwo', view, weight[:, tap_index, :].astype(jnp.float32), precision=lax.Precision.HIGHEST)
    return summed

def reference(hidden, mod_table, timestep, head_weight, conv_in, conv_mid, patch_weight, text_emb):
    per_video = hidden.reshape(VIDEOS, S, D)

    def one_video(packed):
        video_hidden, step_index, video_text = packed
        modulation = mod_table[step_index].astype(jnp.float32)
        gain = 1.0 + modulation[1]
        modulated = (video_hidden.astype(jnp.float32) * gain + modulation[0]).astype(jnp.bfloat16)
        token_out = jnp.dot(modulated, head_weight, preferred_element_type=jnp.float32).astype(jnp.bfloat16)
        latent = token_out.reshape(LT, LH // 2, LW // 2, 2, 2, C).transpose(0, 1, 3, 2, 4, 5).reshape(LT, LH, LW, C)
        pre_first = conv_apply(latent, conv_in, False)
        act_first = jax.nn.silu(pre_first).astype(jnp.bfloat16)
        pre_second = conv_apply(act_first, conv_mid, False)
        decoded = jax.nn.silu(pre_second).astype(jnp.bfloat16)
        pooled = lax.optimization_barrier(jnp.sum(decoded, axis=(1, 2), dtype=jnp.float32)) / (LH * LW)
        reward, pullback = jax.vjp(lambda pool_in: scoring(pool_in, video_text, patch_weight), pooled)
        pool_grad = pullback(jnp.ones((), jnp.float32))[0]
        grad_second = (pool_grad[:, None, None, :] / (LH * LW) * silu_slope(pre_second)).astype(jnp.bfloat16)
        grad_act = conv_apply(grad_second, conv_mid, True)
        grad_first = (grad_act * silu_slope(pre_first)).astype(jnp.bfloat16)
        latent_grad = conv_apply(grad_first, conv_in, True).astype(jnp.bfloat16)
        token_grad = latent_grad.reshape(LT, LH // 2, 2, LW // 2, 2, C).transpose(0, 1, 3, 2, 4, 5).reshape(S, 4 * C)
        hidden_grad = (jnp.dot(token_grad, head_weight.T, preferred_element_type=jnp.float32) * gain).astype(jnp.bfloat16)
        head_term = jnp.dot(modulated.T, token_grad, preferred_element_type=jnp.float32)
        return (reward, hidden_grad, head_term)
    rewards, hidden_grads, head_terms = lax.map(one_video, (per_video, timestep, text_emb))
    return (rewards, lax.optimization_barrier(jnp.sum(head_terms, axis=0)), hidden_grads.reshape(TOKENS, D))
```

```python
import jax
import jax.numpy as jnp
from jax import lax
from jax.experimental import pallas as pl
from jax.experimental.pallas import tpu as pltpu
from jax.sharding import PartitionSpec as P

F32 = jnp.float32
BF16 = jnp.bfloat16
NMP = 32
NDP = 16
FEAT = 160
Q = 32
C = 16
CH = 384
EMB = 1024
CELLS = 4096
SHARD = 48
OWNERS = 8
NT = (((1,), (1,)), ((), ()))


def window_placement():
    source = lax.broadcasted_iota(jnp.int32, (384, 1), 0)
    frame, row, col = (lax.rem(source, 2 * n) // n for n in (64, 32, 16))
    px = 2 * (source // 128) + col - 1
    there = (px >= 0) & (px < 4)
    at = row * 128 + px * 16 + lax.rem(source, 16)
    full = jnp.where(there, at + frame * 64, -1)
    shifted = jnp.where(there & (frame == 0), at + 256 + 64, -1)
    lane = lax.broadcasted_iota(jnp.int32, (384, 512), 1)
    return jnp.where((lane == full) | (lane == shifted), 1.0, 0.0).astype(BF16)


def dot(a, b, dims=(((1,), (0,)), ((), ()))):
    return lax.dot_general(a, b, dims, preferred_element_type=F32)


def sigmoid(value):
    return 1.0 / (1.0 + jnp.exp(-value))


def three_parts(value):
    high = value.astype(BF16)
    rest = value - high.astype(F32)
    middle = rest.astype(BF16)
    low = (rest - middle.astype(F32)).astype(BF16)
    rows = [high.astype(F32), middle.astype(F32), low.astype(F32), jnp.zeros_like(value)]
    return jnp.concatenate(rows, axis=0).astype(BF16)


def from_previous(value):
    rows = value.shape[0]
    inside = lax.rem(lax.broadcasted_iota(jnp.int32, (rows, 1), 0), Q) != 0
    return jnp.where(inside, pltpu.roll(value, 1, 0), 0.0)


def from_next(value):
    rows = value.shape[0]
    inside = lax.rem(lax.broadcasted_iota(jnp.int32, (rows, 1), 0), Q) != Q - 1
    return jnp.where(inside, pltpu.roll(value, rows - 1, 0), 0.0)


def rows_inside(rows, first_row):
    row = lax.broadcasted_iota(jnp.int32, (rows, 1), 0) // Q + first_row
    return jnp.where((row >= 0) & (row < 2 * NMP), 1.0, 0.0).astype(F32)


def spread(ref, frame, even, odd, reverse):
    rows = even.shape[0] // Q
    before_even = from_previous(odd).astype(BF16).reshape(rows, Q, CH)
    after_odd = from_next(even).astype(BF16).reshape(rows, Q, CH)
    even = even.astype(BF16).reshape(rows, Q, CH)
    odd = odd.astype(BF16).reshape(rows, Q, CH)
    low, high = (2, 0) if reverse else (0, 2)
    ref[frame, :, 0:Q, low * CH : (low + 1) * CH] = before_even
    ref[frame, :, 0:Q, CH : 2 * CH] = even
    ref[frame, :, 0:Q, high * CH : (high + 1) * CH] = odd
    ref[frame, :, Q : 2 * Q, low * CH : (low + 1) * CH] = even
    ref[frame, :, Q : 2 * Q, CH : 2 * CH] = odd
    ref[frame, :, Q : 2 * Q, high * CH : (high + 1) * CH] = after_odd


def kernel(
    step_ref,
    hidden_ref,
    mod_ref,
    head_ref,
    cin_ref,
    cmid_ref,
    patch_ref,
    text_ref,
    reward_ref,
    head_grad_ref,
    hidden_grad_ref,
    modulated,
    head_wide,
    place,
    parts_out,
    parts_in,
    latents,
    windows,
    first_weight,
    first_back,
    field,
    second,
    slope_first,
    back_field,
    back_first,
    weights,
    sibling_out,
    sibling_in,
    pooled_all,
    grads,
    hidden_out,
    head_out,
    head_in,
    head_sum,
    sib_sems,
    parts_sems,
    halo_send,
    halo_recv,
    w_send,
    w_recv,
    s_recv,
    pool_sems,
    grad_sems,
    head_sems,
    total_sems,
    out_sem,
):
    dp = lax.axis_index("dp")
    mp = lax.axis_index("mp")
    core = lax.rem(dp, 2)
    x = lax.rem(dp // 2, 4)
    y_hi = dp // 8
    y_lo = lax.rem(mp, 2)
    right_x, left_x, far_x = lax.rem(x + 1, 4), lax.rem(x + 3, 4), lax.rem(x + 2, 4)
    sibling = dp + 1 - 2 * core
    right = y_hi * 8 + right_x * 2 + core
    left = y_hi * 8 + left_x * 2 + core
    other_dp = (1 - y_hi) * 8 + x * 2 + core
    other_mp = mp + 1 - 2 * y_lo
    mine, beside = y_hi * 4, (1 - y_hi) * 4

    def send(src, dst, send_sem, recv_sem, to_dp, to_mp):
        pltpu.make_async_remote_copy(
            src_ref=src,
            dst_ref=dst,
            send_sem=send_sem,
            recv_sem=recv_sem,
            device_id=(to_dp, to_mp),
            device_id_type=pl.DeviceIdType.MESH,
        ).start()

    def wait(ref, sem):
        pltpu.make_async_copy(ref, ref, sem).wait()

    barrier = pltpu.get_barrier_semaphore()

    def greet(to_dp, to_mp):
        pl.semaphore_signal(
            barrier, inc=1, device_id=(to_dp, to_mp), device_id_type=pl.DeviceIdType.MESH
        )

    @pl.loop(1, NMP)
    def _(d):
        greet(dp, lax.rem(mp + d, NMP))

    @pl.loop(1, NDP)
    def _(d):
        greet(lax.rem(dp + d, NDP), mp)

    greet(other_dp, other_mp)

    modulation = mod_ref[step_ref[0]].astype(F32)
    across = lax.broadcasted_iota(jnp.int32, (FEAT, FEAT), 1)
    diagonal = lax.broadcasted_iota(jnp.int32, (FEAT, FEAT), 0) == across
    shift, gain = (
        jnp.sum(jnp.where(diagonal, modulation[n : n + 1], 0.0), axis=1, keepdims=True)
        for n in range(2)
    )
    gain = 1.0 + gain

    @pl.loop(0, 4)
    def _(n):
        halves = []
        for f in range(2):
            columns = pl.ds(pl.multiple_of(n * 256 + f * 1024, 256), 256)
            block = (hidden_ref[:, columns].astype(F32) * gain + shift).astype(BF16)
            modulated[:, columns] = block
            halves.append(dot(head_ref[...], block))
        total = jnp.concatenate(halves, axis=0).T
        parts_out[pl.ds(n * 8, 8)] = total.astype(BF16).reshape(8, Q, 128)

    @pl.loop(0, 18)
    def _(t):
        own = cmid_ref[t + 9].astype(F32)
        sibling_out[t] = jnp.concatenate([own, jnp.zeros((8, CH), F32)], axis=0).astype(BF16)

    pl.semaphore_wait(barrier, NMP - 1 + NDP - 1 + 1)

    send(sibling_out, sibling_in, sib_sems.at[0], sib_sems.at[1], sibling, mp)

    @pl.loop(1, NMP)
    def _(d):
        to = lax.rem(mp + d, NMP)
        send(parts_out.at[to], parts_in.at[NMP - 1 - d], parts_sems.at[0], parts_sems.at[1], dp, to)

    wait(sibling_in, sib_sems.at[1])

    def shard_rows(j):
        return pl.ds(pl.multiple_of(SHARD * j, 16), SHARD)

    own_rows = shard_rows(dp // 2)

    @pl.loop(0, 18)
    def _(t):
        own = sibling_out[t].astype(F32)
        other = sibling_in[t].astype(F32)
        low = jnp.where(core == 0, own, other)
        high = jnp.where(core == 0, other, own)
        weights[t, own_rows, :] = jnp.concatenate([low[0:24], high[0:24]], axis=0).astype(BF16)

    def piece(i, j, c):
        return weights.at[pl.ds(3 * (2 * i + c), 3), shard_rows(j), :]

    def pass_on(i, j, kind, to_dp, to_mp):
        block = piece(i, j, core)
        send(block, block, w_send, w_recv.at[kind, i], to_dp, to_mp)

    def hand_over(i, j, kind):
        block = piece(i, j, core)
        send(block, block, w_send, s_recv.at[kind, i], sibling, mp)

    def arrived(i, j, kind):
        wait(piece(i, j, core), w_recv.at[kind, i])
        hand_over(i, j, kind)

    BESIDE, LEFT, RIGHT, LEFT2, RIGHT2, FAR, FAR2 = range(7)
    own = mine + x
    kinds = (
        (BESIDE, beside + x),
        (LEFT, mine + left_x),
        (RIGHT, mine + right_x),
        (LEFT2, beside + left_x),
        (RIGHT2, beside + right_x),
        (FAR, mine + far_x),
        (FAR2, beside + far_x),
    )
    for i in range(3):
        pass_on(i, own, BESIDE, other_dp, other_mp)
        pass_on(i, own, LEFT, right, mp)
        pass_on(i, own, RIGHT, left, mp)

    first_weight[...] = jnp.zeros_like(first_weight)
    for a in range(2):
        for b in range(3):
            for c in range(3):
                tap = cin_ref[9 + 9 * a + 3 * b + c]
                for j in range(2):
                    at = b * 128 + a * 64 + (c + j) * 16
                    first_weight[at : at + 16, j * CH : (j + 1) * CH] = tap
                at = (a * 3 + b) * 16
                first_back[at : at + 16, c * CH : (c + 1) * CH] = tap

    for f in range(2):
        head_wide[f] = jnp.zeros((FEAT, 128), BF16)
        head_wide[f, :, f * 64 : (f + 1) * 64] = head_ref[...].astype(F32).T.astype(BF16)
    place[...] = window_placement()

    for i in range(3):
        arrived(i, beside + x, BESIDE)
        pass_on(i, beside + x, LEFT2, right, mp)
        pass_on(i, beside + x, RIGHT2, left, mp)
    for i in range(3):
        arrived(i, mine + left_x, LEFT)
        pass_on(i, mine + left_x, FAR, right, mp)
        arrived(i, mine + right_x, RIGHT)

    wait(parts_in, parts_sems.at[1])
    latent = parts_out[mp].astype(F32)
    for s in range(NMP - 1):
        latent = latent + parts_in[s].astype(F32)
    latents[2] = latent.astype(BF16)
    for n, d in enumerate((-2, -1, 1, 2)):
        to = lax.rem(mp + d + NMP, NMP)
        send(latents.at[2], latents.at[2 - d], halo_send.at[n], halo_recv.at[n], dp, to)
    for n, d in enumerate((-2, -1, 1, 2)):
        wait(latents.at[2 - d], halo_recv.at[n])

    pair = lax.broadcasted_iota(jnp.int32, (5 * Q, 1), 0) // Q + mp - 2
    tokens = jnp.where((pair >= 0) & (pair < NMP), latents[...].reshape(5 * Q, 128).astype(F32), 0.0)
    around = jnp.concatenate([from_previous(tokens), tokens, from_next(tokens)], axis=1)
    placed = dot(around.astype(BF16), place[...]).astype(BF16)
    for p in range(5):
        for row in range(2):
            rows = slice(p * Q, (p + 1) * Q)
            windows[1, 2 * p + row] = placed[rows, row * 128 : (row + 1) * 128]
            windows[0, 2 * p + row] = placed[rows, 256 + row * 128 : 256 + (row + 1) * 128]
    for f in range(2):
        taps = jnp.concatenate([windows[f, b : b + 8].reshape(8 * Q, 128) for b in range(3)], axis=1)
        inside = rows_inside(8 * Q, 2 * mp - 3)
        columns = []
        for j in range(2):
            value = dot(taps, first_weight[:, j * CH : (j + 1) * CH])
            gate = sigmoid(value)
            columns.append(value * gate * inside)
            slope = gate * (1.0 + value * (1.0 - gate))
            slope_first[f, :, j * Q : (j + 1) * Q, :] = slope[2 * Q : 6 * Q].reshape(4, Q, CH)
        spread(field, f, columns[0], columns[1], False)

    for i in range(3):
        arrived(i, beside + left_x, LEFT2)
        arrived(i, beside + right_x, RIGHT2)
        pass_on(i, beside + right_x, FAR2, left, mp)
    for i in range(3):
        arrived(i, mine + far_x, FAR)
        arrived(i, beside + far_x, FAR2)

    for i in range(3):
        for kind, j in kinds:
            wait(piece(i, j, 1 - core), s_recv.at[kind, i])
        for g in (2 * i, 2 * i + 1):
            a, b = g // 3, g % 3
            weight = weights[3 * g : 3 * g + 3].reshape(3 * CH, CH)
            for f in range(1 - a, 2):
                source = field[f + a - 1, b : b + 6].reshape(6 * 64, 3 * CH)
                value = dot(source, weight)
                if (g, f) in ((0, 1), (3, 0)):
                    second[f] = value
                else:
                    second[f] = second[f] + value

    pooled_all[mp] = jnp.zeros((8, 128), F32)
    for f in range(2):
        value = second[f, 128:256]
        decoded = (value * sigmoid(value)).astype(BF16).astype(F32)
        sums = jnp.sum(decoded, axis=0, keepdims=True)
        for n in range(3):
            pooled_all[mp, 3 * f + n : 3 * f + n + 1, :] = sums[:, n * 128 : (n + 1) * 128]

    @pl.loop(1, NMP)
    def _(d):
        to = lax.rem(mp + d, NMP)
        send(pooled_all.at[mp], pooled_all.at[mp], pool_sems.at[0], pool_sems.at[1], dp, to)

    row = lax.broadcasted_iota(jnp.int32, (6 * 64, 1), 0) // 64 + 2 * mp - 2
    inside = jnp.where((row >= 0) & (row < 2 * NMP), 1.0, 0.0)
    for f in range(2):
        value = second[f]
        gate = sigmoid(value)
        second[f] = gate * (1.0 + value * (1.0 - gate)) * inside

    wait(pooled_all.at[pl.ds(0, NMP - 1)], pool_sems.at[1])

    sums = pooled_all[0]
    for s in range(1, NMP):
        sums = sums + pooled_all[s]
    sums = sums * (1.0 / CELLS)
    frames = [jnp.concatenate([sums[3 * f + n : 3 * f + n + 1] for n in range(3)], axis=1) for f in range(2)]
    pooled = jnp.concatenate(frames, axis=0)
    rows = dot(three_parts(pooled), patch_ref[...])
    embedded = rows[0:2] + rows[2:4] + rows[4:6]
    text = text_ref[...]
    embed_square = jnp.sum(embedded * embedded, axis=1, keepdims=True) + 1e-6
    embed_scale = lax.rsqrt(embed_square)
    text_scale = lax.rsqrt(jnp.sum(text * text, axis=1, keepdims=True) + 1e-6)
    cosine = jnp.sum(embedded * text, axis=1, keepdims=True) * embed_scale * text_scale
    reward_ref[...] = jnp.broadcast_to(50.0 * (cosine[0:1] + cosine[1:2]), (1, 128))
    embed_grad = 50.0 * embed_scale * (text * text_scale - embedded * (cosine * embed_scale))
    rows = dot(three_parts(embed_grad), patch_ref[...], NT)
    pool_grad = (rows[0:2] + rows[2:4] + rows[4:6]) * (1.0 / CELLS)

    for f in range(2):
        grad = (second[f] * pool_grad[f : f + 1]).reshape(6, 64, CH)
        spread(back_field, f, grad[:, 0:Q].reshape(6 * Q, CH), grad[:, Q:].reshape(6 * Q, CH), True)
    row = lax.broadcasted_iota(jnp.int32, (4 * 64, 1), 0) // 64 + 2 * mp - 1
    inside = jnp.where((row >= 0) & (row < 2 * NMP), 1.0, 0.0)
    for f in range(2):
        total = None
        for a in range(f, 2):
            for b in range(3):
                source = back_field[f + 1 - a, 2 - b : 6 - b].reshape(4 * 64, 3 * CH)
                for c in range(3):
                    term = dot(source[:, c * CH : (c + 1) * CH], weights[9 * a + 3 * b + c], NT)
                    total = term if total is None else total + term
        total = total * slope_first[f].reshape(4 * 64, CH) * inside
        total = total.reshape(4, 64, CH)
        spread(back_first, f, total[:, 0:Q].reshape(4 * Q, CH), total[:, Q:].reshape(4 * Q, CH), True)

    taps = [dot(back_first[f].reshape(4 * 64, 3 * CH), first_back[...], NT) for f in range(2)]
    blocks = []
    for f in range(2):
        for i in range(2):
            for j in range(2):
                total = None
                for a in range(2):
                    if f + 1 - a > 1:
                        continue
                    for b in range(3):
                        at = (i + 2 - b) * 64 + j * Q
                        lane = (a * 3 + b) * 16
                        term = taps[f + 1 - a][at : at + Q, lane : lane + 16]
                        total = term if total is None else total + term
                blocks.append(total)
    grads[mp] = jnp.concatenate(blocks, axis=1).astype(BF16)

    @pl.loop(1, NMP)
    def _(d):
        to = lax.rem(mp + d, NMP)
        send(grads.at[mp], grads.at[mp], grad_sems.at[0], grad_sems.at[1], dp, to)

    wait(grads.at[pl.ds(0, NMP - 1)], grad_sems.at[1])
    token_grad = grads[...].reshape(NMP * Q, 128)

    early = dot(modulated[:, 0:1024], token_grad).T
    late = dot(modulated[:, 1024:2048], token_grad).T
    head_out[...] = early[0:64] + late[64:128]

    @pl.loop(0, OWNERS)
    def _(c):
        @pl.when(c != dp)
        def _():
            block = head_out.at[pl.ds(pl.multiple_of(8 * c, 8), 8)]
            send(block, head_in.at[dp], head_sems.at[0], head_sems.at[1], c, mp)

    def hidden_part(f):
        value = dot(head_wide[f], grads[...].reshape(NMP * Q, 128), NT) * gain
        hidden_out[:, f * 1024 : (f + 1) * 1024] = value.astype(BF16)
        columns = pl.ds(f * 1024, 1024)
        pltpu.make_async_copy(
            hidden_out.at[:, columns], hidden_grad_ref.at[:, columns], out_sem.at[f]
        ).start()

    hidden_part(0)
    own_block = pl.ds(pl.multiple_of(8 * jnp.minimum(dp, OWNERS - 1), 8), 8)

    @pl.when(dp < OWNERS)
    def _():
        head_in[dp] = head_out[own_block, :]
        wait(head_in.at[pl.ds(0, NDP - 1)], head_sems.at[1])
        total = head_in[0]
        for s in range(1, NDP):
            total = total + head_in[s]
        head_sum[own_block, :] = total

        @pl.loop(1, NDP)
        def _(d):
            block = head_sum.at[own_block]
            send(block, block, total_sems.at[0], total_sems.at[1], lax.rem(dp + d, NDP), mp)

    hidden_part(1)

    @pl.when(dp < OWNERS)
    def _():
        wait(head_sum.at[pl.ds(0, 8 * (OWNERS - 1))], total_sems.at[1])
        wait(head_in.at[pl.ds(0, NDP - 1)], total_sems.at[0])
        wait(head_out.at[pl.ds(0, 8 * (OWNERS - 1))], head_sems.at[0])

    @pl.when(dp >= OWNERS)
    def _():
        wait(head_sum, total_sems.at[1])
        wait(head_out, head_sems.at[0])

    head_grad_ref[...] = head_sum[...]

    wait(sibling_out, sib_sems.at[0])
    wait(parts_in, parts_sems.at[0])
    for n in range(4):
        wait(latents.at[2], halo_send.at[n])
    wait(weights.at[:, pl.ds(0, 7 * SHARD), :], w_send)
    wait(pooled_all.at[pl.ds(0, NMP - 1)], pool_sems.at[0])
    wait(grads.at[pl.ds(0, NMP - 1)], grad_sems.at[0])
    for f in range(2):
        columns = pl.ds(f * 1024, 1024)
        pltpu.make_async_copy(
            hidden_out.at[:, columns], hidden_grad_ref.at[:, columns], out_sem.at[f]
        ).wait()


def body(hidden, mod_table, timestep, head_weight, conv_in, conv_mid, patch_weight, text_emb):
    vmem = pl.BlockSpec(memory_space=pltpu.VMEM)
    dma = pltpu.SemaphoreType.DMA
    reward, head_grad, hidden_grad = pl.pallas_call(
        kernel,
        out_shape=(
            jax.ShapeDtypeStruct((1, 128), F32),
            jax.ShapeDtypeStruct((64, FEAT), F32),
            jax.ShapeDtypeStruct((FEAT, 2048), BF16),
        ),
        in_specs=[pl.BlockSpec(memory_space=pltpu.SMEM)] + [vmem] * 7,
        out_specs=(vmem, vmem, pl.BlockSpec(memory_space=pl.ANY)),
        scratch_shapes=[
            pltpu.VMEM((FEAT, 2048), BF16),
            pltpu.VMEM((2, FEAT, 128), BF16),
            pltpu.VMEM((384, 512), BF16),
            pltpu.VMEM((NMP, Q, 128), BF16),
            pltpu.VMEM((NMP - 1, Q, 128), BF16),
            pltpu.VMEM((5, Q, 128), BF16),
            pltpu.VMEM((2, 10, Q, 128), BF16),
            pltpu.VMEM((384, 2 * CH), BF16),
            pltpu.VMEM((96, 3 * CH), BF16),
            pltpu.VMEM((2, 8, 64, 3 * CH), BF16),
            pltpu.VMEM((2, 6 * 64, CH), F32),
            pltpu.VMEM((2, 4, 64, CH), F32),
            pltpu.VMEM((2, 6, 64, 3 * CH), BF16),
            pltpu.VMEM((2, 4, 64, 3 * CH), BF16),
            pltpu.VMEM((18, CH, CH), BF16),
            pltpu.VMEM((18, 32, CH), BF16),
            pltpu.VMEM((18, 32, CH), BF16),
            pltpu.VMEM((NMP, 8, 128), F32),
            pltpu.VMEM((NMP, Q, 128), BF16),
            pltpu.VMEM((FEAT, 2048), BF16),
            pltpu.VMEM((64, FEAT), F32),
            pltpu.VMEM((NDP, 8, FEAT), F32),
            pltpu.VMEM((64, FEAT), F32),
            dma((2,)),
            dma((2,)),
            dma((4,)),
            dma((4,)),
            dma,
            dma((7, 3)),
            dma((7, 3)),
            dma((2,)),
            dma((2,)),
            dma((2,)),
            dma((2,)),
            dma((2,)),
        ],
        compiler_params=pltpu.CompilerParams(
            collective_id=0, has_side_effects=True, vmem_limit_bytes=48 * 1024 * 1024
        ),
        name="guided_step",
    )(
        timestep,
        hidden.T,
        mod_table,
        head_weight.T,
        jnp.transpose(conv_in, (1, 0, 2)),
        jnp.transpose(conv_mid, (1, 0, 2)),
        patch_weight,
        text_emb,
    )
    return (reward[0, 0:1], head_grad.T, hidden_grad.T)


def solution(mesh):
    in_specs = (
        P("dp", "mp"),
        P(None, None, "mp"),
        P("dp"),
        P("mp", None),
        P(),
        P("dp", None, None),
        P(),
        P("dp", None),
    )
    out_specs = (P("dp"), P("mp", None), P("dp", "mp"))
    return jax.shard_map(body, mesh=mesh, in_specs=in_specs, out_specs=out_specs, check_vma=False)
```

```python
import jax
import jax.numpy as jnp
from jax import lax
from jax.experimental import pallas as pl
from jax.experimental.pallas import tpu as pltpu
from jax.sharding import PartitionSpec as P

F32 = jnp.float32
BF16 = jnp.bfloat16
NMP = 32
NDP = 16
FEAT = 160
Q = 32
C = 16
CH = 384
EMB = 1024
CELLS = 4096
SHARD = 48
NEAR = tuple((dz, dy) for dz in (2, 1, -1, 0) for dy in (0, 1) if (dz, dy) != (0, 0))
NT = (((1,), (1,)), ((), ()))


def window_placement():
    source = lax.broadcasted_iota(jnp.int32, (384, 1), 0)
    frame, row, col = (lax.rem(source, 2 * n) // n for n in (64, 32, 16))
    px = 2 * (source // 128) + col - 1
    there = (px >= 0) & (px < 4)
    at = row * 128 + px * 16 + lax.rem(source, 16)
    full = jnp.where(there, at + frame * 64, -1)
    shifted = jnp.where(there & (frame == 0), at + 256 + 64, -1)
    lane = lax.broadcasted_iota(jnp.int32, (384, 512), 1)
    return jnp.where((lane == full) | (lane == shifted), 1.0, 0.0).astype(BF16)


def dot(a, b, dims=(((1,), (0,)), ((), ()))):
    return lax.dot_general(a, b, dims, preferred_element_type=F32)


def sigmoid(value):
    return 1.0 / (1.0 + jnp.exp(-value))


def three_parts(value):
    high = value.astype(BF16)
    rest = value - high.astype(F32)
    middle = rest.astype(BF16)
    low = (rest - middle.astype(F32)).astype(BF16)
    rows = [high.astype(F32), middle.astype(F32), low.astype(F32), jnp.zeros_like(value)]
    return jnp.concatenate(rows, axis=0).astype(BF16)


def from_previous(value):
    rows = value.shape[0]
    inside = lax.rem(lax.broadcasted_iota(jnp.int32, (rows, 1), 0), Q) != 0
    return jnp.where(inside, pltpu.roll(value, 1, 0), 0.0)


def from_next(value):
    rows = value.shape[0]
    inside = lax.rem(lax.broadcasted_iota(jnp.int32, (rows, 1), 0), Q) != Q - 1
    return jnp.where(inside, pltpu.roll(value, rows - 1, 0), 0.0)


def rows_inside(rows, first_row):
    row = lax.broadcasted_iota(jnp.int32, (rows, 1), 0) // Q + first_row
    return jnp.where((row >= 0) & (row < 2 * NMP), 1.0, 0.0).astype(F32)


def spread(ref, frame, even, odd, reverse):
    rows = even.shape[0] // Q
    before_even = from_previous(odd).astype(BF16).reshape(rows, Q, CH)
    after_odd = from_next(even).astype(BF16).reshape(rows, Q, CH)
    even = even.astype(BF16).reshape(rows, Q, CH)
    odd = odd.astype(BF16).reshape(rows, Q, CH)
    low, high = (2, 0) if reverse else (0, 2)
    ref[frame, :, 0:Q, low * CH : (low + 1) * CH] = before_even
    ref[frame, :, 0:Q, CH : 2 * CH] = even
    ref[frame, :, 0:Q, high * CH : (high + 1) * CH] = odd
    ref[frame, :, Q : 2 * Q, low * CH : (low + 1) * CH] = even
    ref[frame, :, Q : 2 * Q, CH : 2 * CH] = odd
    ref[frame, :, Q : 2 * Q, high * CH : (high + 1) * CH] = after_odd


def kernel(
    step_ref,
    hidden_far,
    mod_far,
    head_far,
    cmid_far,
    cin_far,
    patch_far,
    text_far,
    reward_ref,
    head_grad_ref,
    hidden_grad_ref,
    hidden_ref,
    mod_ref,
    head_ref,
    cmid_ref,
    cin_ref,
    patch_ref,
    text_ref,
    modulated,
    head_wide,
    place,
    parts_out,
    parts_in,
    sums_out,
    sums_in,
    own_sum,
    latents,
    windows,
    first_weight,
    first_back,
    field,
    second,
    slope_first,
    back_field,
    back_first,
    weights,
    sibling_out,
    sibling_in,
    pooled_all,
    grads,
    head_in,
    sib_sems,
    parts_send,
    parts_recv,
    sums_sems,
    halo_send,
    halo_recv,
    w_send,
    w_recv,
    s_recv,
    pool_sems,
    far_send,
    far_recv,
    near_sems,
    head_sems,
    in_sems,
):
    dp = lax.axis_index("dp")
    mp = lax.axis_index("mp")
    core = lax.rem(dp, 2)
    x = lax.rem(dp // 2, 4)
    y_hi = dp // 8
    y_lo = lax.rem(mp, 2)
    right_x, left_x, far_x = lax.rem(x + 1, 4), lax.rem(x + 3, 4), lax.rem(x + 2, 4)
    sibling = dp + 1 - 2 * core
    right = y_hi * 8 + right_x * 2 + core
    left = y_hi * 8 + left_x * 2 + core
    other_dp = (1 - y_hi) * 8 + x * 2 + core
    other_mp = mp + 1 - 2 * y_lo
    mine, beside = y_hi * 4, (1 - y_hi) * 4
    z = mp // 2
    block_row, block_column = mp // 8, lax.rem(mp, 8)

    def near(dz, dy):
        return lax.rem(z + dz + 16, 16) * 2 + y_lo + dy * (1 - 2 * y_lo)

    def far(dk):
        return lax.rem(mp + 8 * dk, NMP)

    def send(src, dst, send_sem, recv_sem, to_dp, to_mp):
        pltpu.make_async_remote_copy(
            src_ref=src,
            dst_ref=dst,
            send_sem=send_sem,
            recv_sem=recv_sem,
            device_id=(to_dp, to_mp),
            device_id_type=pl.DeviceIdType.MESH,
        ).start()

    def wait(ref, sem):
        pltpu.make_async_copy(ref, ref, sem).wait()

    loads = [
        pltpu.make_async_copy(far, near, in_sems.at[n])
        for n, (far, near) in enumerate(
            (
                (mod_far, mod_ref),
                (hidden_far, hidden_ref),
                (head_far, head_ref),
                (cmid_far, cmid_ref),
                (cin_far, cin_ref),
                (patch_far, patch_ref),
                (text_far, text_ref),
            )
        )
    ]
    for load in loads:
        load.start()

    barrier = pltpu.get_barrier_semaphore()

    def greet(to_dp, to_mp):
        pl.semaphore_signal(
            barrier, inc=1, device_id=(to_dp, to_mp), device_id_type=pl.DeviceIdType.MESH
        )

    @pl.loop(1, NMP)
    def _(d):
        greet(dp, lax.rem(mp + d, NMP))

    @pl.loop(1, NDP)
    def _(d):
        greet(lax.rem(dp + d, NDP), mp)

    greet(other_dp, other_mp)

    for load in loads[0:4]:
        load.wait()

    modulation = mod_ref[step_ref[0]].astype(F32)
    across = lax.broadcasted_iota(jnp.int32, (FEAT, FEAT), 1)
    diagonal = lax.broadcasted_iota(jnp.int32, (FEAT, FEAT), 0) == across
    shift, gain = (
        jnp.sum(jnp.where(diagonal, modulation[n : n + 1], 0.0), axis=1, keepdims=True)
        for n in range(2)
    )
    gain = 1.0 + gain

    @pl.loop(0, 4)
    def _(n):
        halves = []
        for f in range(2):
            columns = pl.ds(pl.multiple_of(n * 256 + f * 1024, 256), 256)
            block = (hidden_ref[:, columns].astype(F32) * gain + shift).astype(BF16)
            modulated[:, columns] = block
            halves.append(dot(head_ref[...], block))
        total = jnp.concatenate(halves, axis=0).T
        parts_out[n] = total.astype(BF16).reshape(8, Q, 128)

    @pl.loop(0, 18)
    def _(t):
        own = cmid_ref[t + 9].astype(F32)
        sibling_out[t] = jnp.concatenate([own, jnp.zeros((8, CH), F32)], axis=0).astype(BF16)

    pl.semaphore_wait(barrier, NMP - 1 + NDP - 1 + 1)

    send(sibling_out, sibling_in, sib_sems.at[0], sib_sems.at[1], sibling, mp)

    for dk in (2, 1, 3, 0):
        for n, (dz, dy) in enumerate(NEAR):
            to = near(dz, dy)
            block = parts_out.at[lax.rem(to // 8 + dk, 4), lax.rem(to, 8)]
            send(block, parts_in.at[dk, n], parts_send, parts_recv.at[dk], dp, to)

    wait(sibling_in, sib_sems.at[1])

    def shard_rows(j):
        return pl.ds(pl.multiple_of(SHARD * j, 16), SHARD)

    own_rows = shard_rows(dp // 2)

    @pl.loop(0, 18)
    def _(t):
        own = sibling_out[t].astype(F32)
        other = sibling_in[t].astype(F32)
        low = jnp.where(core == 0, own, other)
        high = jnp.where(core == 0, other, own)
        weights[t, own_rows, :] = jnp.concatenate([low[0:24], high[0:24]], axis=0).astype(BF16)

    solo, lent = 1 + y_lo, 2 - y_lo
    SOLO, LENT = 1, 2
    index = (0, solo, lent)

    def piece(slot, j, c):
        return weights.at[pl.ds(3 * (2 * index[slot] + c), 3), shard_rows(j), :]

    def pass_on(slot, j, kind, to_dp, to_mp, to_slot=None):
        block = piece(slot, j, core)
        to_slot = slot if to_slot is None else to_slot
        send(block, block, w_send, w_recv.at[kind, to_slot], to_dp, to_mp)

    def arrived(slot, j, kind):
        wait(piece(slot, j, core), w_recv.at[kind, slot])

    def hand_over(slot, j, kind):
        if slot == SOLO and kind != BESIDE:
            pass_on(slot, j, kind, dp, mp + 1 - 2 * y_lo, LENT)
        block = piece(slot, j, core)
        send(block, block, w_send, s_recv.at[kind, slot], sibling, mp)

    BESIDE, LEFT, RIGHT, LEFT2, RIGHT2, FAR, FAR2 = range(7)
    own = mine + x
    kinds = (
        (BESIDE, beside + x),
        (LEFT, mine + left_x),
        (RIGHT, mine + right_x),
        (LEFT2, beside + left_x),
        (RIGHT2, beside + right_x),
        (FAR, mine + far_x),
        (FAR2, beside + far_x),
    )
    pass_on(LENT, own, BESIDE, other_dp, other_mp, SOLO)
    pass_on(SOLO, own, LEFT, right, mp)
    pass_on(SOLO, own, RIGHT, left, mp)

    def near_sum(dk):
        wait(parts_in.at[dk], parts_recv.at[dk])
        total = parts_out[lax.rem(block_row + dk, 4), block_column].astype(F32)
        for n in range(len(NEAR)):
            total = total + parts_in[dk, n].astype(F32)
        return total

    for dk in (2, 1, 3):
        sums_out[dk - 1] = near_sum(dk).astype(BF16)
        send(sums_out.at[dk - 1], sums_in.at[dk - 1], sums_sems.at[0], sums_sems.at[1], dp, far(dk))
    own_sum[...] = near_sum(0)

    for load in loads[4:7]:
        load.wait()

    arrived(SOLO, beside + x, BESIDE)
    pass_on(SOLO, beside + x, LEFT2, right, mp)
    pass_on(SOLO, beside + x, RIGHT2, left, mp)
    pass_on(0, own, BESIDE, other_dp, other_mp)
    pass_on(0, own, LEFT, right, mp)
    pass_on(0, own, RIGHT, left, mp)
    hand_over(SOLO, beside + x, BESIDE)
    arrived(SOLO, mine + left_x, LEFT)
    pass_on(SOLO, mine + left_x, FAR, right, mp)
    hand_over(SOLO, mine + left_x, LEFT)
    arrived(SOLO, mine + right_x, RIGHT)
    hand_over(SOLO, mine + right_x, RIGHT)
    pass_on(SOLO, own, BESIDE, other_dp, other_mp, LENT)

    first_weight[...] = jnp.zeros_like(first_weight)
    for a in range(2):
        for b in range(3):
            for c in range(3):
                tap = cin_ref[9 + 9 * a + 3 * b + c]
                for j in range(2):
                    at = b * 128 + a * 64 + (c + j) * 16
                    first_weight[at : at + 16, j * CH : (j + 1) * CH] = tap
                at = (a * 3 + b) * 16
                first_back[at : at + 16, c * CH : (c + 1) * CH] = tap

    for f in range(2):
        head_wide[f] = jnp.zeros((FEAT, 128), BF16)
        head_wide[f, :, f * 64 : (f + 1) * 64] = head_ref[...].astype(F32).T.astype(BF16)
    place[...] = window_placement()

    arrived(SOLO, beside + right_x, RIGHT2)
    pass_on(SOLO, beside + right_x, FAR2, left, mp)
    hand_over(SOLO, beside + right_x, RIGHT2)
    arrived(SOLO, beside + left_x, LEFT2)
    hand_over(SOLO, beside + left_x, LEFT2)
    arrived(0, beside + x, BESIDE)
    pass_on(0, beside + x, LEFT2, right, mp)
    pass_on(0, beside + x, RIGHT2, left, mp)
    hand_over(0, beside + x, BESIDE)

    wait(sums_in, sums_sems.at[1])
    latent = own_sum[...]
    for n in range(3):
        latent = latent + sums_in[n].astype(F32)
    latents[2] = latent.astype(BF16)
    for n, d in enumerate((-2, -1, 1, 2)):
        to = lax.rem(mp + d + NMP, NMP)
        send(latents.at[2], latents.at[2 - d], halo_send.at[n], halo_recv.at[n], dp, to)

    arrived(0, mine + left_x, LEFT)
    pass_on(0, mine + left_x, FAR, right, mp)
    hand_over(0, mine + left_x, LEFT)
    arrived(0, mine + right_x, RIGHT)
    hand_over(0, mine + right_x, RIGHT)
    arrived(SOLO, mine + far_x, FAR)
    hand_over(SOLO, mine + far_x, FAR)

    for n, d in enumerate((-2, -1, 1, 2)):
        wait(latents.at[2 - d], halo_recv.at[n])

    pair = lax.broadcasted_iota(jnp.int32, (5 * Q, 1), 0) // Q + mp - 2
    tokens = jnp.where((pair >= 0) & (pair < NMP), latents[...].reshape(5 * Q, 128).astype(F32), 0.0)
    around = jnp.concatenate([from_previous(tokens), tokens, from_next(tokens)], axis=1)
    placed = dot(around.astype(BF16), place[...]).astype(BF16)
    for p in range(5):
        for row in range(2):
            rows = slice(p * Q, (p + 1) * Q)
            windows[1, 2 * p + row] = placed[rows, row * 128 : (row + 1) * 128]
            windows[0, 2 * p + row] = placed[rows, 256 + row * 128 : 256 + (row + 1) * 128]
    for f in range(2):
        taps = jnp.concatenate([windows[f, b : b + 8].reshape(8 * Q, 128) for b in range(3)], axis=1)
        inside = rows_inside(8 * Q, 2 * mp - 3)
        columns = []
        for j in range(2):
            value = dot(taps, first_weight[:, j * CH : (j + 1) * CH])
            gate = sigmoid(value)
            columns.append(value * gate * inside)
            slope = gate * (1.0 + value * (1.0 - gate))
            slope_first[f, :, j * Q : (j + 1) * Q, :] = slope[2 * Q : 6 * Q].reshape(4, Q, CH)
        spread(field, f, columns[0], columns[1], False)

    arrived(SOLO, beside + far_x, FAR2)
    hand_over(SOLO, beside + far_x, FAR2)
    arrived(0, beside + right_x, RIGHT2)
    pass_on(0, beside + right_x, FAR2, left, mp)
    hand_over(0, beside + right_x, RIGHT2)
    arrived(0, beside + left_x, LEFT2)
    hand_over(0, beside + left_x, LEFT2)
    arrived(LENT, beside + x, BESIDE)
    hand_over(LENT, beside + x, BESIDE)
    arrived(0, mine + far_x, FAR)
    hand_over(0, mine + far_x, FAR)
    arrived(0, beside + far_x, FAR2)
    hand_over(0, beside + far_x, FAR2)
    for kind, j in kinds[1:]:
        arrived(LENT, j, kind)
        hand_over(LENT, j, kind)

    for i in range(3):
        for slot in ((0,), (SOLO, LENT), ())[i]:
            for kind, j in kinds:
                wait(piece(slot, j, 1 - core), s_recv.at[kind, slot])
        for g in (2 * i, 2 * i + 1):
            a, b = g // 3, g % 3
            weight = weights[3 * g : 3 * g + 3].reshape(3 * CH, CH)
            for f in range(1 - a, 2):
                source = field[f + a - 1, b : b + 6].reshape(6 * 64, 3 * CH)
                value = dot(source, weight)
                if (g, f) in ((0, 1), (3, 0)):
                    second[f] = value
                else:
                    second[f] = second[f] + value

    for f in range(2):
        value = second[f, 128:256]
        decoded = (value * sigmoid(value)).astype(BF16).astype(F32)
        pooled_all[mp, :, f * CH : (f + 1) * CH] = jnp.sum(decoded, axis=0, keepdims=True)

    @pl.loop(1, NMP)
    def _(d):
        to = lax.rem(mp + d, NMP)
        send(pooled_all.at[mp], pooled_all.at[mp], pool_sems.at[0], pool_sems.at[1], dp, to)

    row = lax.broadcasted_iota(jnp.int32, (6 * 64, 1), 0) // 64 + 2 * mp - 2
    inside = jnp.where((row >= 0) & (row < 2 * NMP), 1.0, 0.0)
    for f in range(2):
        value = second[f]
        gate = sigmoid(value)
        second[f] = gate * (1.0 + value * (1.0 - gate)) * inside

    wait(pooled_all.at[pl.ds(0, NMP - 1)], pool_sems.at[1])

    sums = pooled_all[0]
    for s in range(1, NMP):
        sums = sums + pooled_all[s]
    sums = sums * (1.0 / CELLS)
    pooled = jnp.concatenate([sums[:, 0:CH], sums[:, CH : 2 * CH]], axis=0)
    rows = dot(three_parts(pooled), patch_ref[...])
    embedded = rows[0:2] + rows[2:4] + rows[4:6]
    text = text_ref[...]
    embed_square = jnp.sum(embedded * embedded, axis=1, keepdims=True) + 1e-6
    embed_scale = lax.rsqrt(embed_square)
    text_scale = lax.rsqrt(jnp.sum(text * text, axis=1, keepdims=True) + 1e-6)
    cosine = jnp.sum(embedded * text, axis=1, keepdims=True) * embed_scale * text_scale
    reward_ref[...] = jnp.broadcast_to(50.0 * (cosine[0:1] + cosine[1:2]), (1, 128))
    embed_grad = 50.0 * embed_scale * (text * text_scale - embedded * (cosine * embed_scale))
    rows = dot(three_parts(embed_grad), patch_ref[...], NT)
    pool_grad = (rows[0:2] + rows[2:4] + rows[4:6]) * (1.0 / CELLS)

    for f in range(2):
        grad = (second[f] * pool_grad[f : f + 1]).reshape(6, 64, CH)
        spread(back_field, f, grad[:, 0:Q].reshape(6 * Q, CH), grad[:, Q:].reshape(6 * Q, CH), True)
    row = lax.broadcasted_iota(jnp.int32, (4 * 64, 1), 0) // 64 + 2 * mp - 1
    inside = jnp.where((row >= 0) & (row < 2 * NMP), 1.0, 0.0)
    for f in range(2):
        total = None
        for a in range(f, 2):
            for b in range(3):
                source = back_field[f + 1 - a, 2 - b : 6 - b].reshape(4 * 64, 3 * CH)
                for c in range(3):
                    term = dot(source[:, c * CH : (c + 1) * CH], weights[9 * a + 3 * b + c], NT)
                    total = term if total is None else total + term
        total = total * slope_first[f].reshape(4 * 64, CH) * inside
        total = total.reshape(4, 64, CH)
        spread(back_first, f, total[:, 0:Q].reshape(4 * Q, CH), total[:, Q:].reshape(4 * Q, CH), True)

    taps = [dot(back_first[f].reshape(4 * 64, 3 * CH), first_back[...], NT) for f in range(2)]
    blocks = []
    for f in range(2):
        for i in range(2):
            for j in range(2):
                total = None
                for a in range(2):
                    if f + 1 - a > 1:
                        continue
                    for b in range(3):
                        at = (i + 2 - b) * 64 + j * Q
                        lane = (a * 3 + b) * 16
                        term = taps[f + 1 - a][at : at + Q, lane : lane + 16]
                        total = term if total is None else total + term
                blocks.append(total)
    grads[block_row, block_column] = jnp.concatenate(blocks, axis=1).astype(BF16)

    def spread_near(row):
        block = grads.at[row, block_column]
        for dz, dy in NEAR:
            send(block, block, near_sems.at[0], near_sems.at[1], dp, near(dz, dy))

    for dk in (2, 1, 3):
        block = grads.at[block_row, block_column]
        send(block, block, far_send, far_recv.at[dk - 1], dp, far(dk))
    spread_near(block_row)
    for dk in (1, 3, 2):
        row = lax.rem(block_row + 4 - dk, 4)
        wait(grads.at[row, block_column], far_recv.at[dk - 1])
        spread_near(row)
    wait(grads.at[:, pl.ds(0, 7)], near_sems.at[1])
    token_grad = grads[...].reshape(NMP * Q, 128)

    early = dot(modulated[:, 0:1024], token_grad).T
    late = dot(modulated[:, 1024:2048], token_grad).T
    part = early[0:64] + late[64:128]
    rest = [part[r * 16 : (r + 1) * 16, 128:FEAT] for r in range(4)]
    head_in[dp, 0:64, :] = part[:, 0:128].astype(BF16)
    head_in[dp, 64:80, :] = jnp.concatenate(rest, axis=1).astype(BF16)

    @pl.loop(1, NDP)
    def _(d):
        block = head_in.at[dp]
        send(block, block, head_sems.at[0], head_sems.at[1], lax.rem(dp + d, NDP), mp)

    def hidden_part(f):
        value = dot(head_wide[f], grads[...].reshape(NMP * Q, 128), NT) * gain
        hidden_grad_ref[:, f * 1024 : (f + 1) * 1024] = value.astype(BF16)

    hidden_part(0)
    hidden_part(1)

    wait(head_in.at[pl.ds(0, NDP - 1)], head_sems.at[1])
    total = head_in[0].astype(F32)
    for s in range(1, NDP):
        total = total + head_in[s].astype(F32)
    head_grad_ref[:, 0:128] = total[0:64]
    for r in range(4):
        head_grad_ref[r * 16 : (r + 1) * 16, 128:FEAT] = total[64:80, r * 32 : (r + 1) * 32]

    wait(head_in.at[pl.ds(0, NDP - 1)], head_sems.at[0])
    wait(sibling_out, sib_sems.at[0])
    wait(parts_in, parts_send)
    for n in range(4):
        wait(latents.at[2], halo_send.at[n])
    wait(weights.at[:, pl.ds(0, 7 * SHARD), :], w_send)
    wait(pooled_all.at[pl.ds(0, NMP - 1)], pool_sems.at[0])
    wait(sums_in, sums_sems.at[0])
    wait(grads.at[0, pl.ds(0, 3)], far_send)
    wait(grads.at[:, pl.ds(0, 7)], near_sems.at[0])


def body(hidden, mod_table, timestep, head_weight, conv_in, conv_mid, patch_weight, text_emb):
    vmem = pl.BlockSpec(memory_space=pltpu.VMEM)
    dma = pltpu.SemaphoreType.DMA
    reward, head_grad, hidden_grad = pl.pallas_call(
        kernel,
        out_shape=(
            pltpu.VMEM((1, 128), F32),
            pltpu.VMEM((64, FEAT), F32),
            pltpu.VMEM((FEAT, 2048), BF16),
        ),
        in_specs=[pl.BlockSpec(memory_space=pltpu.SMEM)] + [pl.BlockSpec(memory_space=pltpu.HBM)] * 7,
        out_specs=(vmem, vmem, vmem),
        scratch_shapes=[
            pltpu.VMEM((FEAT, 2048), BF16),
            pltpu.VMEM((50, 2, FEAT), BF16),
            pltpu.VMEM((64, FEAT), BF16),
            pltpu.VMEM((27, 24, CH), BF16),
            pltpu.VMEM((27, C, CH), BF16),
            pltpu.VMEM((CH, EMB), BF16),
            pltpu.VMEM((1, EMB), F32),
            pltpu.VMEM((FEAT, 2048), BF16),
            pltpu.VMEM((2, FEAT, 128), BF16),
            pltpu.VMEM((384, 512), BF16),
            pltpu.VMEM((4, 8, Q, 128), BF16),
            pltpu.VMEM((4, 7, Q, 128), BF16),
            pltpu.VMEM((3, Q, 128), BF16),
            pltpu.VMEM((3, Q, 128), BF16),
            pltpu.VMEM((Q, 128), F32),
            pltpu.VMEM((5, Q, 128), BF16),
            pltpu.VMEM((2, 10, Q, 128), BF16),
            pltpu.VMEM((384, 2 * CH), BF16),
            pltpu.VMEM((96, 3 * CH), BF16),
            pltpu.VMEM((2, 8, 64, 3 * CH), BF16),
            pltpu.VMEM((2, 6 * 64, CH), F32),
            pltpu.VMEM((2, 4, 64, CH), F32),
            pltpu.VMEM((2, 6, 64, 3 * CH), BF16),
            pltpu.VMEM((2, 4, 64, 3 * CH), BF16),
            pltpu.VMEM((18, CH, CH), BF16),
            pltpu.VMEM((18, 32, CH), BF16),
            pltpu.VMEM((18, 32, CH), BF16),
            pltpu.VMEM((NMP, 1, 2 * CH), F32),
            pltpu.VMEM((4, 8, Q, 128), BF16),
            pltpu.VMEM((NDP, 80, 128), BF16),
            dma((2,)),
            dma,
            dma((4,)),
            dma((2,)),
            dma((4,)),
            dma((4,)),
            dma,
            dma((7, 3)),
            dma((7, 3)),
            dma((2,)),
            dma,
            dma((3,)),
            dma((2,)),
            dma((2,)),
            dma((7,)),
        ],
        compiler_params=pltpu.CompilerParams(
            collective_id=0, has_side_effects=True, vmem_limit_bytes=48 * 1024 * 1024
        ),
        name="guided_step",
    )(
        timestep,
        *(
            pltpu.with_memory_space_constraint(operand, pltpu.HBM)
            for operand in (
                hidden.T,
                mod_table,
                head_weight.T,
                jnp.transpose(conv_mid, (1, 0, 2)),
                jnp.transpose(conv_in, (1, 0, 2)),
                patch_weight,
                text_emb,
            )
        ),
    )
    return (reward[0, 0:1], head_grad.T, hidden_grad.T)


def solution(mesh):
    in_specs = (
        P("dp", "mp"),
        P(None, None, "mp"),
        P("dp"),
        P("mp", None),
        P(),
        P("dp", None, None),
        P(),
        P("dp", None),
    )
    out_specs = (P("dp"), P("mp", None), P("dp", "mp"))
    return jax.shard_map(body, mesh=mesh, in_specs=in_specs, out_specs=out_specs, check_vma=False)
```

```python
import jax
import jax.numpy as jnp
from jax import lax
from jax.experimental import pallas as pl
from jax.experimental.pallas import tpu as pltpu
from jax.sharding import PartitionSpec as P

F32 = jnp.float32
BF16 = jnp.bfloat16
NMP = 32
NDP = 16
FEAT = 160
Q = 32
C = 16
CH = 384
EMB = 1024
CELLS = 4096
SHARD = 48
NEAR = tuple((dz, dy) for dz in (2, 1, -1, 0) for dy in (0, 1) if (dz, dy) != (0, 0))
NT = (((1,), (1,)), ((), ()))


def window_placement():
    source = lax.broadcasted_iota(jnp.int32, (384, 1), 0)
    frame, row, col = (lax.rem(source, 2 * n) // n for n in (64, 32, 16))
    px = 2 * (source // 128) + col - 1
    there = (px >= 0) & (px < 4)
    at = row * 128 + px * 16 + lax.rem(source, 16)
    full = jnp.where(there, at + frame * 64, -1)
    shifted = jnp.where(there & (frame == 0), at + 256 + 64, -1)
    lane = lax.broadcasted_iota(jnp.int32, (384, 512), 1)
    return jnp.where((lane == full) | (lane == shifted), 1.0, 0.0).astype(BF16)


def dot(a, b, dims=(((1,), (0,)), ((), ()))):
    return lax.dot_general(a, b, dims, preferred_element_type=F32)


def sigmoid(value):
    return 1.0 / (1.0 + jnp.exp(-value))


def three_parts(value):
    high = value.astype(BF16)
    rest = value - high.astype(F32)
    middle = rest.astype(BF16)
    low = (rest - middle.astype(F32)).astype(BF16)
    rows = [high.astype(F32), middle.astype(F32), low.astype(F32), jnp.zeros_like(value)]
    return jnp.concatenate(rows, axis=0).astype(BF16)


def from_previous(value):
    rows = value.shape[0]
    inside = lax.rem(lax.broadcasted_iota(jnp.int32, (rows, 1), 0), Q) != 0
    return jnp.where(inside, pltpu.roll(value, 1, 0), 0.0)


def from_next(value):
    rows = value.shape[0]
    inside = lax.rem(lax.broadcasted_iota(jnp.int32, (rows, 1), 0), Q) != Q - 1
    return jnp.where(inside, pltpu.roll(value, rows - 1, 0), 0.0)


def rows_inside(rows, first_row):
    row = lax.broadcasted_iota(jnp.int32, (rows, 1), 0) // Q + first_row
    return jnp.where((row >= 0) & (row < 2 * NMP), 1.0, 0.0).astype(F32)


def spread(ref, frame, even, odd, reverse):
    rows = even.shape[0] // Q
    before_even = from_previous(odd).astype(BF16).reshape(rows, Q, CH)
    after_odd = from_next(even).astype(BF16).reshape(rows, Q, CH)
    even = even.astype(BF16).reshape(rows, Q, CH)
    odd = odd.astype(BF16).reshape(rows, Q, CH)
    low, high = (2, 0) if reverse else (0, 2)
    ref[frame, :, 0:Q, low * CH : (low + 1) * CH] = before_even
    ref[frame, :, 0:Q, CH : 2 * CH] = even
    ref[frame, :, 0:Q, high * CH : (high + 1) * CH] = odd
    ref[frame, :, Q : 2 * Q, low * CH : (low + 1) * CH] = even
    ref[frame, :, Q : 2 * Q, CH : 2 * CH] = odd
    ref[frame, :, Q : 2 * Q, high * CH : (high + 1) * CH] = after_odd


def kernel(
    step_ref,
    hidden_far,
    mod_far,
    head_far,
    cmid_far,
    cin_far,
    patch_far,
    text_far,
    reward_ref,
    head_grad_ref,
    hidden_grad_ref,
    hidden_ref,
    mod_ref,
    head_ref,
    cmid_ref,
    cin_ref,
    patch_ref,
    text_ref,
    modulated,
    head_wide,
    place,
    parts_out,
    parts_in,
    sums_out,
    sums_in,
    own_sum,
    latents,
    windows,
    first_weight,
    first_back,
    field,
    second,
    slope_first,
    back_field,
    back_first,
    weights,
    sibling_out,
    sibling_in,
    pooled_all,
    grads,
    head_in,
    sib_sems,
    parts_send,
    parts_recv,
    sums_sems,
    halo_send,
    halo_recv,
    w_send,
    w_recv,
    s_recv,
    pool_sems,
    far_send,
    far_recv,
    near_sems,
    head_sems,
    in_sems,
):
    dp = lax.axis_index("dp")
    mp = lax.axis_index("mp")
    core = lax.rem(dp, 2)
    x = lax.rem(dp // 2, 4)
    y_hi = dp // 8
    y_lo = lax.rem(mp, 2)
    right_x, left_x, far_x = lax.rem(x + 1, 4), lax.rem(x + 3, 4), lax.rem(x + 2, 4)
    sibling = dp + 1 - 2 * core
    right = y_hi * 8 + right_x * 2 + core
    left = y_hi * 8 + left_x * 2 + core
    other_dp = (1 - y_hi) * 8 + x * 2 + core
    other_mp = mp + 1 - 2 * y_lo
    mine, beside = y_hi * 4, (1 - y_hi) * 4
    z = mp // 2
    block_row, block_column = mp // 8, lax.rem(mp, 8)

    def near(dz, dy):
        return lax.rem(z + dz + 16, 16) * 2 + y_lo + dy * (1 - 2 * y_lo)

    def far(dk):
        return lax.rem(mp + 8 * dk, NMP)

    def send(src, dst, send_sem, recv_sem, to_dp, to_mp):
        pltpu.make_async_remote_copy(
            src_ref=src,
            dst_ref=dst,
            send_sem=send_sem,
            recv_sem=recv_sem,
            device_id=(to_dp, to_mp),
            device_id_type=pl.DeviceIdType.MESH,
        ).start()

    def wait(ref, sem):
        pltpu.make_async_copy(ref, ref, sem).wait()

    loads = [
        pltpu.make_async_copy(far, near, in_sems.at[n])
        for n, (far, near) in enumerate(
            (
                (cmid_far, cmid_ref),
                (mod_far, mod_ref),
                (hidden_far, hidden_ref),
                (head_far, head_ref),
                (cin_far, cin_ref),
                (patch_far, patch_ref),
                (text_far, text_ref),
            )
        )
    ]
    for load in loads:
        load.start()

    barrier = pltpu.get_barrier_semaphore()

    def greet(to_dp, to_mp):
        pl.semaphore_signal(
            barrier, inc=1, device_id=(to_dp, to_mp), device_id_type=pl.DeviceIdType.MESH
        )

    @pl.loop(1, NMP)
    def _(d):
        greet(dp, lax.rem(mp + d, NMP))

    @pl.loop(1, NDP)
    def _(d):
        greet(lax.rem(dp + d, NDP), mp)

    greet(other_dp, other_mp)

    loads[0].wait()

    @pl.loop(0, 18)
    def _(t):
        own = cmid_ref[t + 9].astype(F32)
        sibling_out[t] = jnp.concatenate([own, jnp.zeros((8, CH), F32)], axis=0).astype(BF16)

    pl.semaphore_wait(barrier, NMP - 1 + NDP - 1 + 1)

    send(sibling_out, sibling_in, sib_sems.at[0], sib_sems.at[1], sibling, mp)

    for load in loads[1:4]:
        load.wait()

    modulation = mod_ref[step_ref[0]].astype(F32)
    across = lax.broadcasted_iota(jnp.int32, (FEAT, FEAT), 1)
    diagonal = lax.broadcasted_iota(jnp.int32, (FEAT, FEAT), 0) == across
    shift, gain = (
        jnp.sum(jnp.where(diagonal, modulation[n : n + 1], 0.0), axis=1, keepdims=True)
        for n in range(2)
    )
    gain = 1.0 + gain

    @pl.loop(0, 4)
    def _(n):
        halves = []
        for f in range(2):
            columns = pl.ds(pl.multiple_of(n * 256 + f * 1024, 256), 256)
            block = (hidden_ref[:, columns].astype(F32) * gain + shift).astype(BF16)
            modulated[:, columns] = block
            halves.append(dot(head_ref[...], block))
        total = jnp.concatenate(halves, axis=0).T
        parts_out[n] = total.astype(BF16).reshape(8, Q, 128)

    for dk in (2, 1, 3, 0):
        for n, (dz, dy) in enumerate(NEAR):
            to = near(dz, dy)
            block = parts_out.at[lax.rem(to // 8 + dk, 4), lax.rem(to, 8)]
            send(block, parts_in.at[dk, n], parts_send, parts_recv.at[dk], dp, to)

    wait(sibling_in, sib_sems.at[1])

    def shard_rows(j):
        return pl.ds(pl.multiple_of(SHARD * j, 16), SHARD)

    own_rows = shard_rows(dp // 2)

    @pl.loop(0, 18)
    def _(t):
        own = sibling_out[t].astype(F32)
        other = sibling_in[t].astype(F32)
        low = jnp.where(core == 0, own, other)
        high = jnp.where(core == 0, other, own)
        weights[t, own_rows, :] = jnp.concatenate([low[0:24], high[0:24]], axis=0).astype(BF16)

    solo, lent = 1 + y_lo, 2 - y_lo
    SOLO, LENT = 1, 2
    index = (0, solo, lent)

    def piece(slot, j, c):
        return weights.at[pl.ds(3 * (2 * index[slot] + c), 3), shard_rows(j), :]

    def pass_on(slot, j, kind, to_dp, to_mp, to_slot=None):
        block = piece(slot, j, core)
        to_slot = slot if to_slot is None else to_slot
        send(block, block, w_send, w_recv.at[kind, to_slot], to_dp, to_mp)

    def arrived(slot, j, kind):
        wait(piece(slot, j, core), w_recv.at[kind, slot])

    def hand_over(slot, j, kind):
        if slot == SOLO and kind != BESIDE:
            pass_on(slot, j, kind, dp, mp + 1 - 2 * y_lo, LENT)
        if slot == 0 and kind in (LEFT, RIGHT, FAR):
            pass_on(slot, j, {LEFT: LEFT2, RIGHT: RIGHT2, FAR: FAR2}[kind], other_dp, other_mp)
        block = piece(slot, j, core)
        send(block, block, w_send, s_recv.at[kind, slot], sibling, mp)

    BESIDE, LEFT, RIGHT, LEFT2, RIGHT2, FAR, FAR2 = range(7)
    own = mine + x
    kinds = (
        (BESIDE, beside + x),
        (LEFT, mine + left_x),
        (RIGHT, mine + right_x),
        (LEFT2, beside + left_x),
        (RIGHT2, beside + right_x),
        (FAR, mine + far_x),
        (FAR2, beside + far_x),
    )
    pass_on(LENT, own, BESIDE, other_dp, other_mp, SOLO)
    pass_on(SOLO, own, LEFT, right, mp)
    pass_on(SOLO, own, RIGHT, left, mp)
    pass_on(0, own, LEFT, right, mp)
    pass_on(0, own, RIGHT, left, mp)

    for load in loads[4:7]:
        load.wait()

    first_weight[...] = jnp.zeros_like(first_weight)
    for a in range(2):
        for b in range(3):
            for c in range(3):
                tap = cin_ref[9 + 9 * a + 3 * b + c]
                for j in range(2):
                    at = b * 128 + a * 64 + (c + j) * 16
                    first_weight[at : at + 16, j * CH : (j + 1) * CH] = tap
                at = (a * 3 + b) * 16
                first_back[at : at + 16, c * CH : (c + 1) * CH] = tap

    for f in range(2):
        head_wide[f] = jnp.zeros((FEAT, 128), BF16)
        head_wide[f, :, f * 64 : (f + 1) * 64] = head_ref[...].astype(F32).T.astype(BF16)
    place[...] = window_placement()

    def near_sum(dk):
        wait(parts_in.at[dk], parts_recv.at[dk])
        total = parts_out[lax.rem(block_row + dk, 4), block_column].astype(F32)
        for n in range(len(NEAR)):
            total = total + parts_in[dk, n].astype(F32)
        return total

    for dk in (2, 1, 3):
        sums_out[dk - 1] = near_sum(dk).astype(BF16)
        send(sums_out.at[dk - 1], sums_in.at[dk - 1], sums_sems.at[0], sums_sems.at[1], dp, far(dk))
    own_sum[...] = near_sum(0)

    arrived(SOLO, beside + x, BESIDE)
    pass_on(SOLO, beside + x, LEFT2, right, mp)
    pass_on(SOLO, beside + x, RIGHT2, left, mp)
    hand_over(SOLO, beside + x, BESIDE)
    arrived(SOLO, mine + left_x, LEFT)
    pass_on(SOLO, mine + left_x, FAR, right, mp)
    hand_over(SOLO, mine + left_x, LEFT)
    arrived(SOLO, mine + right_x, RIGHT)
    hand_over(SOLO, mine + right_x, RIGHT)
    pass_on(0, own, BESIDE, other_dp, other_mp)
    pass_on(SOLO, own, BESIDE, other_dp, other_mp, LENT)
    arrived(0, mine + left_x, LEFT)
    pass_on(0, mine + left_x, FAR, right, mp)
    hand_over(0, mine + left_x, LEFT)
    arrived(0, mine + right_x, RIGHT)
    hand_over(0, mine + right_x, RIGHT)

    arrived(SOLO, beside + right_x, RIGHT2)
    pass_on(SOLO, beside + right_x, FAR2, left, mp)
    hand_over(SOLO, beside + right_x, RIGHT2)
    arrived(SOLO, beside + left_x, LEFT2)
    hand_over(SOLO, beside + left_x, LEFT2)

    wait(sums_in, sums_sems.at[1])
    latent = own_sum[...]
    for n in range(3):
        latent = latent + sums_in[n].astype(F32)
    latents[2] = latent.astype(BF16)
    for n, d in enumerate((-2, -1, 1, 2)):
        to = lax.rem(mp + d + NMP, NMP)
        send(latents.at[2], latents.at[2 - d], halo_send.at[n], halo_recv.at[n], dp, to)

    arrived(SOLO, mine + far_x, FAR)
    hand_over(SOLO, mine + far_x, FAR)
    arrived(0, mine + far_x, FAR)
    hand_over(0, mine + far_x, FAR)
    arrived(SOLO, beside + far_x, FAR2)
    hand_over(SOLO, beside + far_x, FAR2)
    arrived(0, beside + x, BESIDE)
    hand_over(0, beside + x, BESIDE)
    arrived(LENT, beside + x, BESIDE)
    hand_over(LENT, beside + x, BESIDE)

    for n, d in enumerate((-2, -1, 1, 2)):
        wait(latents.at[2 - d], halo_recv.at[n])

    pair = lax.broadcasted_iota(jnp.int32, (5 * Q, 1), 0) // Q + mp - 2
    tokens = jnp.where((pair >= 0) & (pair < NMP), latents[...].reshape(5 * Q, 128).astype(F32), 0.0)
    around = jnp.concatenate([from_previous(tokens), tokens, from_next(tokens)], axis=1)
    placed = dot(around.astype(BF16), place[...]).astype(BF16)
    for p in range(5):
        for row in range(2):
            rows = slice(p * Q, (p + 1) * Q)
            windows[1, 2 * p + row] = placed[rows, row * 128 : (row + 1) * 128]
            windows[0, 2 * p + row] = placed[rows, 256 + row * 128 : 256 + (row + 1) * 128]
    for f in range(2):
        taps = jnp.concatenate([windows[f, b : b + 8].reshape(8 * Q, 128) for b in range(3)], axis=1)
        inside = rows_inside(8 * Q, 2 * mp - 3)
        columns = []
        for j in range(2):
            value = dot(taps, first_weight[:, j * CH : (j + 1) * CH])
            gate = sigmoid(value)
            columns.append(value * gate * inside)
            slope = gate * (1.0 + value * (1.0 - gate))
            slope_first[f, :, j * Q : (j + 1) * Q, :] = slope[2 * Q : 6 * Q].reshape(4, Q, CH)
        spread(field, f, columns[0], columns[1], False)

    for kind, j in kinds[1:]:
        if kind in (LEFT2, RIGHT2, FAR2):
            arrived(0, j, kind)
            hand_over(0, j, kind)
        arrived(LENT, j, kind)
        hand_over(LENT, j, kind)
    for slot in range(3):
        for kind, j in kinds:
            wait(piece(slot, j, 1 - core), s_recv.at[kind, slot])

    def tap(a, b):
        at = 9 * a + 3 * b
        return weights[at : at + 3].reshape(3 * CH, CH)

    def middle(starts):
        early, late = None, None
        for b in range(3):
            both = jnp.concatenate([tap(1, b), tap(0, b)], axis=1)
            sources = [
                jnp.concatenate([field[f, r + b : r + b + 2].reshape(128, 3 * CH) for r in starts], axis=0)
                for f in range(2)
            ]
            terms = dot(sources[0], both), dot(sources[1], tap(1, b))
            early = terms[0] if early is None else early + terms[0]
            late = terms[1] if late is None else late + terms[1]
        late = late + early[:, CH : 2 * CH]
        for n, r in enumerate(starts):
            second[0, r * 64 : r * 64 + 128] = early[n * 128 : (n + 1) * 128, 0:CH]
            second[1, r * 64 : r * 64 + 128] = late[n * 128 : (n + 1) * 128]

    middle((2,))

    for f in range(2):
        value = second[f, 128:256]
        decoded = (value * sigmoid(value)).astype(BF16).astype(F32)
        pooled_all[mp, :, f * CH : (f + 1) * CH] = jnp.sum(decoded, axis=0, keepdims=True)

    @pl.loop(1, NMP)
    def _(d):
        to = lax.rem(mp + d, NMP)
        send(pooled_all.at[mp], pooled_all.at[mp], pool_sems.at[0], pool_sems.at[1], dp, to)

    middle((0, 4))
    row = lax.broadcasted_iota(jnp.int32, (6 * 64, 1), 0) // 64 + 2 * mp - 2
    inside = jnp.where((row >= 0) & (row < 2 * NMP), 1.0, 0.0)
    for f in range(2):
        value = second[f]
        gate = sigmoid(value)
        second[f] = gate * (1.0 + value * (1.0 - gate)) * inside

    wait(pooled_all.at[pl.ds(0, NMP - 1)], pool_sems.at[1])

    sums = pooled_all[0]
    for s in range(1, NMP):
        sums = sums + pooled_all[s]
    sums = sums * (1.0 / CELLS)
    pooled = jnp.concatenate([sums[:, 0:CH], sums[:, CH : 2 * CH]], axis=0)
    rows = dot(three_parts(pooled), patch_ref[...])
    embedded = rows[0:2] + rows[2:4] + rows[4:6]
    text = text_ref[...]
    embed_square = jnp.sum(embedded * embedded, axis=1, keepdims=True) + 1e-6
    embed_scale = lax.rsqrt(embed_square)
    text_scale = lax.rsqrt(jnp.sum(text * text, axis=1, keepdims=True) + 1e-6)
    cosine = jnp.sum(embedded * text, axis=1, keepdims=True) * embed_scale * text_scale
    reward_ref[...] = jnp.broadcast_to(50.0 * (cosine[0:1] + cosine[1:2]), (1, 128))
    embed_grad = 50.0 * embed_scale * (text * text_scale - embedded * (cosine * embed_scale))
    rows = dot(three_parts(embed_grad), patch_ref[...], NT)
    pool_grad = (rows[0:2] + rows[2:4] + rows[4:6]) * (1.0 / CELLS)

    for f in range(2):
        grad = (second[f] * pool_grad[f : f + 1]).reshape(6, 64, CH)
        spread(back_field, f, grad[:, 0:Q].reshape(6 * Q, CH), grad[:, Q:].reshape(6 * Q, CH), True)
    row = lax.broadcasted_iota(jnp.int32, (4 * 64, 1), 0) // 64 + 2 * mp - 1
    inside = jnp.where((row >= 0) & (row < 2 * NMP), 1.0, 0.0)
    late, early = None, None
    for b in range(3):
        sources = [back_field[f, 2 - b : 6 - b].reshape(4 * 64, 3 * CH) for f in range(2)]
        both = [
            jnp.concatenate([weights[9 * a + 3 * b + c] for c in range(3)], axis=1) for a in range(2)
        ]
        terms = dot(sources[1], jnp.concatenate([both[1], both[0]], axis=0), NT), dot(sources[0], both[1], NT)
        late = terms[0] if late is None else late + terms[0]
        early = terms[1] if early is None else early + terms[1]
    grad_field = (early + late[:, CH : 2 * CH], late[:, 0:CH])
    for f in range(2):
        total = grad_field[f]
        total = total * slope_first[f].reshape(4 * 64, CH) * inside
        total = total.reshape(4, 64, CH)
        spread(back_first, f, total[:, 0:Q].reshape(4 * Q, CH), total[:, Q:].reshape(4 * Q, CH), True)

    taps = [dot(back_first[f].reshape(4 * 64, 3 * CH), first_back[...], NT) for f in range(2)]
    blocks = []
    for f in range(2):
        for i in range(2):
            for j in range(2):
                total = None
                for a in range(2):
                    if f + 1 - a > 1:
                        continue
                    for b in range(3):
                        at = (i + 2 - b) * 64 + j * Q
                        lane = (a * 3 + b) * 16
                        term = taps[f + 1 - a][at : at + Q, lane : lane + 16]
                        total = term if total is None else total + term
                blocks.append(total)
    grads[block_row, block_column] = jnp.concatenate(blocks, axis=1).astype(BF16)

    def spread_near(row):
        block = grads.at[row, block_column]
        for dz, dy in NEAR:
            send(block, block, near_sems.at[0], near_sems.at[1], dp, near(dz, dy))

    for dk in (2, 1, 3):
        block = grads.at[block_row, block_column]
        send(block, block, far_send, far_recv.at[dk - 1], dp, far(dk))
    spread_near(block_row)
    for dk in (1, 3, 2):
        row = lax.rem(block_row + 4 - dk, 4)
        wait(grads.at[row, block_column], far_recv.at[dk - 1])
        spread_near(row)
    wait(grads.at[:, pl.ds(0, 7)], near_sems.at[1])
    token_grad = grads[...].reshape(NMP * Q, 128)

    early = dot(modulated[:, 0:1024], token_grad).T
    late = dot(modulated[:, 1024:2048], token_grad).T
    part = early[0:64] + late[64:128]
    rest = [part[r * 16 : (r + 1) * 16, 128:FEAT] for r in range(4)]
    head_in[dp, 0:64, :] = part[:, 0:128].astype(BF16)
    head_in[dp, 64:80, :] = jnp.concatenate(rest, axis=1).astype(BF16)

    @pl.loop(1, NDP)
    def _(d):
        block = head_in.at[dp]
        send(block, block, head_sems.at[0], head_sems.at[1], lax.rem(dp + d, NDP), mp)

    def hidden_part(f):
        value = dot(head_wide[f], grads[...].reshape(NMP * Q, 128), NT) * gain
        hidden_grad_ref[:, f * 1024 : (f + 1) * 1024] = value.astype(BF16)

    hidden_part(0)
    hidden_part(1)

    wait(head_in.at[pl.ds(0, NDP - 1)], head_sems.at[1])
    total = head_in[0].astype(F32)
    for s in range(1, NDP):
        total = total + head_in[s].astype(F32)
    head_grad_ref[:, 0:128] = total[0:64]
    for r in range(4):
        head_grad_ref[r * 16 : (r + 1) * 16, 128:FEAT] = total[64:80, r * 32 : (r + 1) * 32]

    wait(head_in.at[pl.ds(0, NDP - 1)], head_sems.at[0])
    wait(sibling_out, sib_sems.at[0])
    wait(parts_in, parts_send)
    for n in range(4):
        wait(latents.at[2], halo_send.at[n])
    wait(weights.at[:, pl.ds(0, 7 * SHARD), :], w_send)
    wait(pooled_all.at[pl.ds(0, NMP - 1)], pool_sems.at[0])
    wait(sums_in, sums_sems.at[0])
    wait(grads.at[0, pl.ds(0, 3)], far_send)
    wait(grads.at[:, pl.ds(0, 7)], near_sems.at[0])


def body(hidden, mod_table, timestep, head_weight, conv_in, conv_mid, patch_weight, text_emb):
    vmem = pl.BlockSpec(memory_space=pltpu.VMEM)
    dma = pltpu.SemaphoreType.DMA
    reward, head_grad, hidden_grad = pl.pallas_call(
        kernel,
        out_shape=(
            pltpu.VMEM((1, 128), F32),
            pltpu.VMEM((64, FEAT), F32),
            pltpu.VMEM((FEAT, 2048), BF16),
        ),
        in_specs=[pl.BlockSpec(memory_space=pltpu.SMEM)] + [pl.BlockSpec(memory_space=pltpu.HBM)] * 7,
        out_specs=(vmem, vmem, vmem),
        scratch_shapes=[
            pltpu.VMEM((FEAT, 2048), BF16),
            pltpu.VMEM((50, 2, FEAT), BF16),
            pltpu.VMEM((64, FEAT), BF16),
            pltpu.VMEM((27, 24, CH), BF16),
            pltpu.VMEM((27, C, CH), BF16),
            pltpu.VMEM((CH, EMB), BF16),
            pltpu.VMEM((1, EMB), F32),
            pltpu.VMEM((FEAT, 2048), BF16),
            pltpu.VMEM((2, FEAT, 128), BF16),
            pltpu.VMEM((384, 512), BF16),
            pltpu.VMEM((4, 8, Q, 128), BF16),
            pltpu.VMEM((4, 7, Q, 128), BF16),
            pltpu.VMEM((3, Q, 128), BF16),
            pltpu.VMEM((3, Q, 128), BF16),
            pltpu.VMEM((Q, 128), F32),
            pltpu.VMEM((5, Q, 128), BF16),
            pltpu.VMEM((2, 10, Q, 128), BF16),
            pltpu.VMEM((384, 2 * CH), BF16),
            pltpu.VMEM((96, 3 * CH), BF16),
            pltpu.VMEM((2, 8, 64, 3 * CH), BF16),
            pltpu.VMEM((2, 6 * 64, CH), F32),
            pltpu.VMEM((2, 4, 64, CH), F32),
            pltpu.VMEM((2, 6, 64, 3 * CH), BF16),
            pltpu.VMEM((2, 4, 64, 3 * CH), BF16),
            pltpu.VMEM((18, CH, CH), BF16),
            pltpu.VMEM((18, 32, CH), BF16),
            pltpu.VMEM((18, 32, CH), BF16),
            pltpu.VMEM((NMP, 1, 2 * CH), F32),
            pltpu.VMEM((4, 8, Q, 128), BF16),
            pltpu.VMEM((NDP, 80, 128), BF16),
            dma((2,)),
            dma,
            dma((4,)),
            dma((2,)),
            dma((4,)),
            dma((4,)),
            dma,
            dma((7, 3)),
            dma((7, 3)),
            dma((2,)),
            dma,
            dma((3,)),
            dma((2,)),
            dma((2,)),
            dma((7,)),
        ],
        compiler_params=pltpu.CompilerParams(
            collective_id=0, has_side_effects=True, vmem_limit_bytes=48 * 1024 * 1024
        ),
        name="guided_step",
    )(
        timestep,
        *(
            pltpu.with_memory_space_constraint(operand, pltpu.HBM)
            for operand in (
                hidden.T,
                mod_table,
                head_weight.T,
                jnp.transpose(conv_mid, (1, 0, 2)),
                jnp.transpose(conv_in, (1, 0, 2)),
                patch_weight,
                text_emb,
            )
        ),
    )
    return (reward[0, 0:1], head_grad.T, hidden_grad.T)


def solution(mesh):
    in_specs = (
        P("dp", "mp"),
        P(None, None, "mp"),
        P("dp"),
        P("mp", None),
        P(),
        P("dp", None, None),
        P(),
        P("dp", None),
    )
    out_specs = (P("dp"), P("mp", None), P("dp", "mp"))
    return jax.shard_map(body, mesh=mesh, in_specs=in_specs, out_specs=out_specs, check_vma=False)
```

```python
import jax
import jax.numpy as jnp
from jax import lax
from jax.experimental import pallas as pl
from jax.experimental.pallas import tpu as pltpu
from jax.sharding import PartitionSpec as P

F32 = jnp.float32
BF16 = jnp.bfloat16
NMP = 32
NDP = 16
FEAT = 160
Q = 32
C = 16
CH = 384
EMB = 1024
CELLS = 4096
SHARD = 48
NEAR = tuple((dz, dy) for dz in (2, 1, -1, 0) for dy in (0, 1) if (dz, dy) != (0, 0))
NT = (((1,), (1,)), ((), ()))


def window_placement():
    source = lax.broadcasted_iota(jnp.int32, (384, 1), 0)
    frame, row, col = (lax.rem(source, 2 * n) // n for n in (64, 32, 16))
    px = 2 * (source // 128) + col - 1
    there = (px >= 0) & (px < 4)
    at = row * 128 + px * 16 + lax.rem(source, 16)
    full = jnp.where(there, at + frame * 64, -1)
    shifted = jnp.where(there & (frame == 0), at + 256 + 64, -1)
    lane = lax.broadcasted_iota(jnp.int32, (384, 512), 1)
    return jnp.where((lane == full) | (lane == shifted), 1.0, 0.0).astype(BF16)


def dot(a, b, dims=(((1,), (0,)), ((), ()))):
    return lax.dot_general(a, b, dims, preferred_element_type=F32)


def sigmoid(value):
    return 1.0 / (1.0 + jnp.exp(-value))


def three_parts(value):
    high = value.astype(BF16)
    rest = value - high.astype(F32)
    middle = rest.astype(BF16)
    low = (rest - middle.astype(F32)).astype(BF16)
    rows = [high.astype(F32), middle.astype(F32), low.astype(F32), jnp.zeros_like(value)]
    return jnp.concatenate(rows, axis=0).astype(BF16)


def from_previous(value):
    rows = value.shape[0]
    inside = lax.rem(lax.broadcasted_iota(jnp.int32, (rows, 1), 0), Q) != 0
    return jnp.where(inside, pltpu.roll(value, 1, 0), 0.0)


def from_next(value):
    rows = value.shape[0]
    inside = lax.rem(lax.broadcasted_iota(jnp.int32, (rows, 1), 0), Q) != Q - 1
    return jnp.where(inside, pltpu.roll(value, rows - 1, 0), 0.0)


def rows_inside(rows, first_row):
    row = lax.broadcasted_iota(jnp.int32, (rows, 1), 0) // Q + first_row
    return jnp.where((row >= 0) & (row < 2 * NMP), 1.0, 0.0).astype(F32)


def spread(ref, frame, even, odd, reverse):
    rows = even.shape[0] // Q
    before_even = from_previous(odd).astype(BF16).reshape(rows, Q, CH)
    after_odd = from_next(even).astype(BF16).reshape(rows, Q, CH)
    even = even.astype(BF16).reshape(rows, Q, CH)
    odd = odd.astype(BF16).reshape(rows, Q, CH)
    low, high = (2, 0) if reverse else (0, 2)
    ref[frame, :, 0:Q, low * CH : (low + 1) * CH] = before_even
    ref[frame, :, 0:Q, CH : 2 * CH] = even
    ref[frame, :, 0:Q, high * CH : (high + 1) * CH] = odd
    ref[frame, :, Q : 2 * Q, low * CH : (low + 1) * CH] = even
    ref[frame, :, Q : 2 * Q, CH : 2 * CH] = odd
    ref[frame, :, Q : 2 * Q, high * CH : (high + 1) * CH] = after_odd


def kernel(
    step_ref,
    hidden_far,
    mod_far,
    head_far,
    cmid_far,
    cin_far,
    patch_far,
    text_far,
    reward_ref,
    head_grad_ref,
    hidden_grad_ref,
    hidden_ref,
    mod_ref,
    head_ref,
    cmid_ref,
    cin_ref,
    patch_ref,
    text_ref,
    modulated,
    head_wide,
    place,
    parts_out,
    parts_in,
    sums_out,
    sums_in,
    own_sum,
    latents,
    windows,
    first_weight,
    first_back,
    field,
    second,
    slope_first,
    back_field,
    back_first,
    weights,
    sibling_out,
    sibling_in,
    pooled_all,
    grads,
    head_in,
    sib_sems,
    parts_send,
    parts_recv,
    sums_sems,
    halo_send,
    halo_recv,
    w_send,
    w_recv,
    s_recv,
    pool_sems,
    far_send,
    far_recv,
    near_sems,
    head_sems,
    in_sems,
):
    dp = lax.axis_index("dp")
    mp = lax.axis_index("mp")
    core = lax.rem(dp, 2)
    x = lax.rem(dp // 2, 4)
    y_hi = dp // 8
    y_lo = lax.rem(mp, 2)
    right_x, left_x, far_x = lax.rem(x + 1, 4), lax.rem(x + 3, 4), lax.rem(x + 2, 4)
    sibling = dp + 1 - 2 * core
    right = y_hi * 8 + right_x * 2 + core
    left = y_hi * 8 + left_x * 2 + core
    other_dp = (1 - y_hi) * 8 + x * 2 + core
    other_mp = mp + 1 - 2 * y_lo
    mine, beside = y_hi * 4, (1 - y_hi) * 4
    z = mp // 2
    block_row, block_column = mp // 8, lax.rem(mp, 8)

    def near(dz, dy):
        return lax.rem(z + dz + 16, 16) * 2 + y_lo + dy * (1 - 2 * y_lo)

    def far(dk):
        return lax.rem(mp + 8 * dk, NMP)

    def send(src, dst, send_sem, recv_sem, to_dp, to_mp):
        pltpu.make_async_remote_copy(
            src_ref=src,
            dst_ref=dst,
            send_sem=send_sem,
            recv_sem=recv_sem,
            device_id=(to_dp, to_mp),
            device_id_type=pl.DeviceIdType.MESH,
        ).start()

    def wait(ref, sem):
        pltpu.make_async_copy(ref, ref, sem).wait()

    barrier = pltpu.get_barrier_semaphore()

    def greet(to_dp, to_mp):
        pl.semaphore_signal(
            barrier, inc=1, device_id=(to_dp, to_mp), device_id_type=pl.DeviceIdType.MESH
        )

    @pl.loop(1, NMP)
    def _(d):
        greet(dp, lax.rem(mp + d, NMP))

    @pl.loop(1, NDP)
    def _(d):
        greet(lax.rem(dp + d, NDP), mp)

    greet(other_dp, other_mp)

    loads = [
        pltpu.make_async_copy(far, near, in_sems.at[n])
        for n, (far, near) in enumerate(
            (
                (cmid_far, cmid_ref),
                (mod_far, mod_ref),
                (hidden_far, hidden_ref),
                (head_far, head_ref),
                (cin_far, cin_ref),
                (patch_far, patch_ref),
                (text_far, text_ref),
            )
        )
    ]
    for load in loads:
        load.start()

    loads[0].wait()

    @pl.loop(0, 18)
    def _(t):
        own = cmid_ref[t + 9].astype(F32)
        sibling_out[t] = jnp.concatenate([own, jnp.zeros((8, CH), F32)], axis=0).astype(BF16)

    pl.semaphore_wait(barrier, NMP - 1 + NDP - 1 + 1)

    send(sibling_out, sibling_in, sib_sems.at[0], sib_sems.at[1], sibling, mp)

    for load in loads[1:4]:
        load.wait()

    modulation = mod_ref[step_ref[0]].astype(F32)
    across = lax.broadcasted_iota(jnp.int32, (FEAT, FEAT), 1)
    diagonal = lax.broadcasted_iota(jnp.int32, (FEAT, FEAT), 0) == across
    shift, gain = (
        jnp.sum(jnp.where(diagonal, modulation[n : n + 1], 0.0), axis=1, keepdims=True)
        for n in range(2)
    )
    gain = 1.0 + gain

    @pl.loop(0, 4)
    def _(n):
        halves = []
        for f in range(2):
            columns = pl.ds(pl.multiple_of(n * 256 + f * 1024, 256), 256)
            block = (hidden_ref[:, columns].astype(F32) * gain + shift).astype(BF16)
            modulated[:, columns] = block
            halves.append(dot(head_ref[...], block))
        total = jnp.concatenate(halves, axis=0).T
        parts_out[n] = total.astype(BF16).reshape(8, Q, 128)

    for dk in (2, 1, 3, 0):
        for n, (dz, dy) in enumerate(NEAR):
            to = near(dz, dy)
            block = parts_out.at[lax.rem(to // 8 + dk, 4), lax.rem(to, 8)]
            send(block, parts_in.at[dk, n], parts_send, parts_recv.at[dk], dp, to)

    wait(sibling_in, sib_sems.at[1])

    def shard_rows(j):
        return pl.ds(pl.multiple_of(SHARD * j, 16), SHARD)

    own_rows = shard_rows(dp // 2)

    @pl.loop(0, 18)
    def _(t):
        own = sibling_out[t].astype(F32)
        other = sibling_in[t].astype(F32)
        low = jnp.where(core == 0, own, other)
        high = jnp.where(core == 0, other, own)
        weights[t, own_rows, :] = jnp.concatenate([low[0:24], high[0:24]], axis=0).astype(BF16)

    z_odd = lax.rem(z, 2)
    solo = 1 + lax.rem(y_lo + z, 2)
    lent = 3 - solo
    SOLO, LENT = 1, 2
    index = (0, solo, lent)

    def piece(slot, j, c):
        return weights.at[pl.ds(3 * (2 * index[slot] + c), 3), shard_rows(j), :]

    def part(slot, j, t):
        return weights.at[3 * (2 * index[slot] + core) + t, shard_rows(j), :]

    def pass_on(slot, j, kind, to_dp, to_mp, to_slot=None):
        to_slot = slot if to_slot is None else to_slot
        for t in range(3):
            block = part(slot, j, t)
            send(block, block, w_send, w_recv.at[kind, to_slot, t], to_dp, to_mp)

    def relay(slot, j, kind, *onward):
        if slot == SOLO and kind in (LEFT, RIGHT, FAR2):
            onward += ((kind, LENT, dp, mp + 1 - 2 * y_lo),)
        elif slot == SOLO:
            onward += ((kind, LENT, dp, mp + 2 - 4 * z_odd),)
        if slot == 0 and kind in (LEFT, RIGHT, FAR):
            onward += (({LEFT: LEFT2, RIGHT: RIGHT2, FAR: FAR2}[kind], 0, other_dp, other_mp),)
        for t in range(3):
            block = part(slot, j, t)
            wait(block, w_recv.at[kind, slot, t])
            for to_kind, to_slot, to_dp, to_mp, *only in onward:
                if only and t not in only[0]:
                    continue
                send(block, block, w_send, w_recv.at[to_kind, to_slot, t], to_dp, to_mp)
            send(block, block, w_send, s_recv.at[kind, slot], sibling, mp)

    BESIDE, LEFT, RIGHT, LEFT2, RIGHT2, FAR, FAR2 = range(7)
    own = mine + x
    kinds = (
        (BESIDE, beside + x),
        (LEFT, mine + left_x),
        (RIGHT, mine + right_x),
        (LEFT2, beside + left_x),
        (RIGHT2, beside + right_x),
        (FAR, mine + far_x),
        (FAR2, beside + far_x),
    )
    pass_on(LENT, own, BESIDE, other_dp, other_mp, SOLO)
    pass_on(SOLO, own, LEFT, right, mp)
    pass_on(SOLO, own, RIGHT, left, mp)
    pass_on(0, own, LEFT, right, mp)
    pass_on(0, own, RIGHT, left, mp)

    for load in loads[4:7]:
        load.wait()

    first_weight[...] = jnp.zeros_like(first_weight)
    for a in range(2):
        for b in range(3):
            for c in range(3):
                tap = cin_ref[9 + 9 * a + 3 * b + c]
                for j in range(2):
                    at = b * 128 + a * 64 + (c + j) * 16
                    first_weight[at : at + 16, j * CH : (j + 1) * CH] = tap
                at = (a * 3 + b) * 16
                first_back[at : at + 16, c * CH : (c + 1) * CH] = tap

    for f in range(2):
        head_wide[f] = jnp.zeros((FEAT, 128), BF16)
        head_wide[f, :, f * 64 : (f + 1) * 64] = head_ref[...].astype(F32).T.astype(BF16)
    place[...] = window_placement()

    def near_sum(dk):
        wait(parts_in.at[dk], parts_recv.at[dk])
        total = parts_out[lax.rem(block_row + dk, 4), block_column].astype(F32)
        for n in range(len(NEAR)):
            total = total + parts_in[dk, n].astype(F32)
        return total

    for dk in (2, 1, 3):
        sums_out[dk - 1] = near_sum(dk).astype(BF16)
        send(sums_out.at[dk - 1], sums_in.at[dk - 1], sums_sems.at[0], sums_sems.at[1], dp, far(dk))
    own_sum[...] = near_sum(0)

    relay(SOLO, beside + x, BESIDE, (LEFT2, SOLO, right, mp), (RIGHT2, SOLO, left, mp))
    relay(SOLO, mine + left_x, LEFT, (FAR, SOLO, right, mp))
    relay(SOLO, mine + right_x, RIGHT)
    pass_on(0, own, BESIDE, other_dp, other_mp)
    relay(0, mine + left_x, LEFT, (FAR, 0, right, mp, (0, 1)))
    relay(0, mine + right_x, RIGHT, (FAR, 0, left, mp, (2,)))

    relay(SOLO, beside + right_x, RIGHT2, (FAR2, SOLO, left, mp))
    relay(SOLO, beside + left_x, LEFT2)

    wait(sums_in, sums_sems.at[1])
    latent = own_sum[...]
    for n in range(3):
        latent = latent + sums_in[n].astype(F32)
    latents[2] = latent.astype(BF16)
    for n, d in enumerate((-2, -1, 1, 2)):
        to = lax.rem(mp + d + NMP, NMP)
        send(latents.at[2], latents.at[2 - d], halo_send.at[n], halo_recv.at[n], dp, to)

    relay(SOLO, mine + far_x, FAR)
    relay(0, mine + far_x, FAR)
    relay(SOLO, beside + far_x, FAR2)
    relay(0, beside + x, BESIDE)
    relay(LENT, beside + x, BESIDE)

    for n, d in enumerate((-2, -1, 1, 2)):
        wait(latents.at[2 - d], halo_recv.at[n])

    pair = lax.broadcasted_iota(jnp.int32, (5 * Q, 1), 0) // Q + mp - 2
    tokens = jnp.where((pair >= 0) & (pair < NMP), latents[...].reshape(5 * Q, 128).astype(F32), 0.0)
    around = jnp.concatenate([from_previous(tokens), tokens, from_next(tokens)], axis=1)
    placed = dot(around.astype(BF16), place[...]).astype(BF16)
    for p in range(5):
        for row in range(2):
            rows = slice(p * Q, (p + 1) * Q)
            windows[1, 2 * p + row] = placed[rows, row * 128 : (row + 1) * 128]
            windows[0, 2 * p + row] = placed[rows, 256 + row * 128 : 256 + (row + 1) * 128]
    for f in range(2):
        taps = jnp.concatenate([windows[f, b : b + 8].reshape(8 * Q, 128) for b in range(3)], axis=1)
        inside = rows_inside(8 * Q, 2 * mp - 3)
        columns = []
        for j in range(2):
            value = dot(taps, first_weight[:, j * CH : (j + 1) * CH])
            gate = sigmoid(value)
            columns.append(value * gate * inside)
            slope = gate * (1.0 + value * (1.0 - gate))
            slope_first[f, :, j * Q : (j + 1) * Q, :] = slope[2 * Q : 6 * Q].reshape(4, Q, CH)
        spread(field, f, columns[0], columns[1], False)

    for kind, j in kinds[1:]:
        if kind in (LEFT2, RIGHT2, FAR2):
            relay(0, j, kind)
        relay(LENT, j, kind)
    for slot in range(3):
        for kind, j in kinds:
            wait(piece(slot, j, 1 - core), s_recv.at[kind, slot])

    def tap(a, b):
        at = 9 * a + 3 * b
        return weights[at : at + 3].reshape(3 * CH, CH)

    def middle(starts):
        early, late = None, None
        for b in range(3):
            both = jnp.concatenate([tap(1, b), tap(0, b)], axis=1)
            sources = [
                jnp.concatenate([field[f, r + b : r + b + 2].reshape(128, 3 * CH) for r in starts], axis=0)
                for f in range(2)
            ]
            terms = dot(sources[0], both), dot(sources[1], tap(1, b))
            early = terms[0] if early is None else early + terms[0]
            late = terms[1] if late is None else late + terms[1]
        late = late + early[:, CH : 2 * CH]
        for n, r in enumerate(starts):
            second[0, r * 64 : r * 64 + 128] = early[n * 128 : (n + 1) * 128, 0:CH]
            second[1, r * 64 : r * 64 + 128] = late[n * 128 : (n + 1) * 128]

    middle((2,))

    for f in range(2):
        value = second[f, 128:256]
        decoded = (value * sigmoid(value)).astype(BF16).astype(F32)
        pooled_all[mp, :, f * CH : (f + 1) * CH] = jnp.sum(decoded, axis=0, keepdims=True)

    @pl.loop(1, NMP)
    def _(d):
        to = lax.rem(mp + d, NMP)
        send(pooled_all.at[mp], pooled_all.at[mp], pool_sems.at[0], pool_sems.at[1], dp, to)

    middle((0, 4))
    row = lax.broadcasted_iota(jnp.int32, (6 * 64, 1), 0) // 64 + 2 * mp - 2
    inside = jnp.where((row >= 0) & (row < 2 * NMP), 1.0, 0.0)
    for f in range(2):
        value = second[f]
        gate = sigmoid(value)
        second[f] = gate * (1.0 + value * (1.0 - gate)) * inside

    wait(pooled_all.at[pl.ds(0, NMP - 1)], pool_sems.at[1])

    sums = pooled_all[0]
    for s in range(1, NMP):
        sums = sums + pooled_all[s]
    sums = sums * (1.0 / CELLS)
    pooled = jnp.concatenate([sums[:, 0:CH], sums[:, CH : 2 * CH]], axis=0)
    rows = dot(three_parts(pooled), patch_ref[...])
    embedded = rows[0:2] + rows[2:4] + rows[4:6]
    text = text_ref[...]
    embed_square = jnp.sum(embedded * embedded, axis=1, keepdims=True) + 1e-6
    embed_scale = lax.rsqrt(embed_square)
    text_scale = lax.rsqrt(jnp.sum(text * text, axis=1, keepdims=True) + 1e-6)
    cosine = jnp.sum(embedded * text, axis=1, keepdims=True) * embed_scale * text_scale
    reward_ref[...] = jnp.broadcast_to(50.0 * (cosine[0:1] + cosine[1:2]), (1, 128))
    embed_grad = 50.0 * embed_scale * (text * text_scale - embedded * (cosine * embed_scale))
    rows = dot(three_parts(embed_grad), patch_ref[...], NT)
    pool_grad = (rows[0:2] + rows[2:4] + rows[4:6]) * (1.0 / CELLS)

    for f in range(2):
        grad = (second[f] * pool_grad[f : f + 1]).reshape(6, 64, CH)
        spread(back_field, f, grad[:, 0:Q].reshape(6 * Q, CH), grad[:, Q:].reshape(6 * Q, CH), True)
    row = lax.broadcasted_iota(jnp.int32, (4 * 64, 1), 0) // 64 + 2 * mp - 1
    inside = jnp.where((row >= 0) & (row < 2 * NMP), 1.0, 0.0)
    late, early = None, None
    for b in range(3):
        sources = [back_field[f, 2 - b : 6 - b].reshape(4 * 64, 3 * CH) for f in range(2)]
        both = [
            jnp.concatenate([weights[9 * a + 3 * b + c] for c in range(3)], axis=1) for a in range(2)
        ]
        terms = dot(sources[1], jnp.concatenate([both[1], both[0]], axis=0), NT), dot(sources[0], both[1], NT)
        late = terms[0] if late is None else late + terms[0]
        early = terms[1] if early is None else early + terms[1]
    grad_field = (early + late[:, CH : 2 * CH], late[:, 0:CH])
    for f in range(2):
        total = grad_field[f]
        total = total * slope_first[f].reshape(4 * 64, CH) * inside
        total = total.reshape(4, 64, CH)
        spread(back_first, f, total[:, 0:Q].reshape(4 * Q, CH), total[:, Q:].reshape(4 * Q, CH), True)

    taps = [dot(back_first[f].reshape(4 * 64, 3 * CH), first_back[...], NT) for f in range(2)]
    blocks = []
    for f in range(2):
        for i in range(2):
            for j in range(2):
                total = None
                for a in range(2):
                    if f + 1 - a > 1:
                        continue
                    for b in range(3):
                        at = (i + 2 - b) * 64 + j * Q
                        lane = (a * 3 + b) * 16
                        term = taps[f + 1 - a][at : at + Q, lane : lane + 16]
                        total = term if total is None else total + term
                blocks.append(total)
    grads[block_row, block_column] = jnp.concatenate(blocks, axis=1).astype(BF16)

    def spread_near(row):
        block = grads.at[row, block_column]
        for dz, dy in NEAR:
            send(block, block, near_sems.at[0], near_sems.at[1], dp, near(dz, dy))

    for dk in (2, 1, 3):
        block = grads.at[block_row, block_column]
        send(block, block, far_send, far_recv.at[dk - 1], dp, far(dk))
    spread_near(block_row)
    for dk in (1, 3, 2):
        row = lax.rem(block_row + 4 - dk, 4)
        wait(grads.at[row, block_column], far_recv.at[dk - 1])
        spread_near(row)
    wait(grads.at[:, pl.ds(0, 7)], near_sems.at[1])
    token_grad = grads[...].reshape(NMP * Q, 128)

    early = dot(modulated[:, 0:1024], token_grad).T
    late = dot(modulated[:, 1024:2048], token_grad).T
    part = early[0:64] + late[64:128]
    rest = [part[r * 16 : (r + 1) * 16, 128:FEAT] for r in range(4)]
    head_in[dp, 0:64, :] = part[:, 0:128].astype(BF16)
    head_in[dp, 64:80, :] = jnp.concatenate(rest, axis=1).astype(BF16)

    @pl.loop(1, NDP)
    def _(d):
        block = head_in.at[dp]
        send(block, block, head_sems.at[0], head_sems.at[1], lax.rem(dp + d, NDP), mp)

    def hidden_part(f):
        value = dot(head_wide[f], grads[...].reshape(NMP * Q, 128), NT) * gain
        hidden_grad_ref[:, f * 1024 : (f + 1) * 1024] = value.astype(BF16)

    hidden_part(0)
    hidden_part(1)

    wait(head_in.at[pl.ds(0, NDP - 1)], head_sems.at[1])
    total = head_in[0].astype(F32)
    for s in range(1, NDP):
        total = total + head_in[s].astype(F32)
    head_grad_ref[:, 0:128] = total[0:64]
    for r in range(4):
        head_grad_ref[r * 16 : (r + 1) * 16, 128:FEAT] = total[64:80, r * 32 : (r + 1) * 32]

    wait(head_in.at[pl.ds(0, NDP - 1)], head_sems.at[0])
    wait(sibling_out, sib_sems.at[0])
    wait(parts_in, parts_send)
    for n in range(4):
        wait(latents.at[2], halo_send.at[n])
    wait(weights.at[:, pl.ds(0, 7 * SHARD), :], w_send)
    wait(pooled_all.at[pl.ds(0, NMP - 1)], pool_sems.at[0])
    wait(sums_in, sums_sems.at[0])
    wait(grads.at[0, pl.ds(0, 3)], far_send)
    wait(grads.at[:, pl.ds(0, 7)], near_sems.at[0])


def body(hidden, mod_table, timestep, head_weight, conv_in, conv_mid, patch_weight, text_emb):
    vmem = pl.BlockSpec(memory_space=pltpu.VMEM)
    dma = pltpu.SemaphoreType.DMA
    reward, head_grad, hidden_grad = pl.pallas_call(
        kernel,
        out_shape=(
            pltpu.VMEM((1, 128), F32),
            pltpu.VMEM((64, FEAT), F32),
            pltpu.VMEM((FEAT, 2048), BF16),
        ),
        in_specs=[pl.BlockSpec(memory_space=pltpu.SMEM)] + [pl.BlockSpec(memory_space=pltpu.HBM)] * 7,
        out_specs=(vmem, vmem, vmem),
        scratch_shapes=[
            pltpu.VMEM((FEAT, 2048), BF16),
            pltpu.VMEM((50, 2, FEAT), BF16),
            pltpu.VMEM((64, FEAT), BF16),
            pltpu.VMEM((27, 24, CH), BF16),
            pltpu.VMEM((27, C, CH), BF16),
            pltpu.VMEM((CH, EMB), BF16),
            pltpu.VMEM((1, EMB), F32),
            pltpu.VMEM((FEAT, 2048), BF16),
            pltpu.VMEM((2, FEAT, 128), BF16),
            pltpu.VMEM((384, 512), BF16),
            pltpu.VMEM((4, 8, Q, 128), BF16),
            pltpu.VMEM((4, 7, Q, 128), BF16),
            pltpu.VMEM((3, Q, 128), BF16),
            pltpu.VMEM((3, Q, 128), BF16),
            pltpu.VMEM((Q, 128), F32),
            pltpu.VMEM((5, Q, 128), BF16),
            pltpu.VMEM((2, 10, Q, 128), BF16),
            pltpu.VMEM((384, 2 * CH), BF16),
            pltpu.VMEM((96, 3 * CH), BF16),
            pltpu.VMEM((2, 8, 64, 3 * CH), BF16),
            pltpu.VMEM((2, 6 * 64, CH), F32),
            pltpu.VMEM((2, 4, 64, CH), F32),
            pltpu.VMEM((2, 6, 64, 3 * CH), BF16),
            pltpu.VMEM((2, 4, 64, 3 * CH), BF16),
            pltpu.VMEM((18, CH, CH), BF16),
            pltpu.VMEM((18, 32, CH), BF16),
            pltpu.VMEM((18, 32, CH), BF16),
            pltpu.VMEM((NMP, 1, 2 * CH), F32),
            pltpu.VMEM((4, 8, Q, 128), BF16),
            pltpu.VMEM((NDP, 80, 128), BF16),
            dma((2,)),
            dma,
            dma((4,)),
            dma((2,)),
            dma((4,)),
            dma((4,)),
            dma,
            dma((7, 3, 3)),
            dma((7, 3)),
            dma((2,)),
            dma,
            dma((3,)),
            dma((2,)),
            dma((2,)),
            dma((7,)),
        ],
        compiler_params=pltpu.CompilerParams(
            collective_id=0, has_side_effects=True, vmem_limit_bytes=48 * 1024 * 1024
        ),
        name="guided_step",
    )(
        timestep,
        *(
            pltpu.with_memory_space_constraint(operand, pltpu.HBM)
            for operand in (
                hidden.T,
                mod_table,
                head_weight.T,
                jnp.transpose(conv_mid, (1, 0, 2)),
                jnp.transpose(conv_in, (1, 0, 2)),
                patch_weight,
                text_emb,
            )
        ),
    )
    return (reward[0, 0:1], head_grad.T, hidden_grad.T)


def solution(mesh):
    in_specs = (
        P("dp", "mp"),
        P(None, None, "mp"),
        P("dp"),
        P("mp", None),
        P(),
        P("dp", None, None),
        P(),
        P("dp", None),
    )
    out_specs = (P("dp"), P("mp", None), P("dp", "mp"))
    return jax.shard_map(body, mesh=mesh, in_specs=in_specs, out_specs=out_specs, check_vma=False)
```

```python
import jax
import jax.numpy as jnp
from jax import lax
from jax.experimental import pallas as pl
from jax.experimental.pallas import tpu as pltpu
from jax.sharding import PartitionSpec as P

F32 = jnp.float32
BF16 = jnp.bfloat16
NMP = 32
NDP = 16
FEAT = 160
Q = 32
C = 16
CH = 384
EMB = 1024
CELLS = 4096
SHARD = 48
NEAR = tuple((dz, dy) for dz in (2, 1, -1, 0) for dy in (0, 1) if (dz, dy) != (0, 0))
NT = (((1,), (1,)), ((), ()))


def window_placement():
    source = lax.broadcasted_iota(jnp.int32, (384, 1), 0)
    frame, row, col = (lax.rem(source, 2 * n) // n for n in (64, 32, 16))
    px = 2 * (source // 128) + col - 1
    there = (px >= 0) & (px < 4)
    at = row * 128 + px * 16 + lax.rem(source, 16)
    full = jnp.where(there, at + frame * 64, -1)
    shifted = jnp.where(there & (frame == 0), at + 256 + 64, -1)
    lane = lax.broadcasted_iota(jnp.int32, (384, 512), 1)
    return jnp.where((lane == full) | (lane == shifted), 1.0, 0.0).astype(BF16)


def dot(a, b, dims=(((1,), (0,)), ((), ()))):
    return lax.dot_general(a, b, dims, preferred_element_type=F32)


def sigmoid(value):
    return 1.0 / (1.0 + jnp.exp(-value))


def three_parts(value):
    high = value.astype(BF16)
    rest = value - high.astype(F32)
    middle = rest.astype(BF16)
    low = (rest - middle.astype(F32)).astype(BF16)
    rows = [high.astype(F32), middle.astype(F32), low.astype(F32), jnp.zeros_like(value)]
    return jnp.concatenate(rows, axis=0).astype(BF16)


def from_previous(value):
    rows = value.shape[0]
    inside = lax.rem(lax.broadcasted_iota(jnp.int32, (rows, 1), 0), Q) != 0
    return jnp.where(inside, pltpu.roll(value, 1, 0), 0.0)


def from_next(value):
    rows = value.shape[0]
    inside = lax.rem(lax.broadcasted_iota(jnp.int32, (rows, 1), 0), Q) != Q - 1
    return jnp.where(inside, pltpu.roll(value, rows - 1, 0), 0.0)


def rows_inside(rows, first_row):
    row = lax.broadcasted_iota(jnp.int32, (rows, 1), 0) // Q + first_row
    return jnp.where((row >= 0) & (row < 2 * NMP), 1.0, 0.0).astype(F32)


def spread(ref, frame, even, odd, reverse):
    rows = even.shape[0] // Q
    before_even = from_previous(odd).astype(BF16).reshape(rows, Q, CH)
    after_odd = from_next(even).astype(BF16).reshape(rows, Q, CH)
    even = even.astype(BF16).reshape(rows, Q, CH)
    odd = odd.astype(BF16).reshape(rows, Q, CH)
    low, high = (2, 0) if reverse else (0, 2)
    ref[frame, :, 0:Q, low * CH : (low + 1) * CH] = before_even
    ref[frame, :, 0:Q, CH : 2 * CH] = even
    ref[frame, :, 0:Q, high * CH : (high + 1) * CH] = odd
    ref[frame, :, Q : 2 * Q, low * CH : (low + 1) * CH] = even
    ref[frame, :, Q : 2 * Q, CH : 2 * CH] = odd
    ref[frame, :, Q : 2 * Q, high * CH : (high + 1) * CH] = after_odd


def kernel(
    step_ref,
    hidden_far,
    mod_far,
    head_far,
    cmid_far,
    cin_far,
    patch_far,
    text_far,
    reward_ref,
    head_grad_ref,
    hidden_grad_ref,
    hidden_ref,
    mod_ref,
    head_ref,
    cmid_ref,
    cin_ref,
    patch_ref,
    text_ref,
    modulated,
    head_wide,
    place,
    parts_out,
    parts_in,
    sums_out,
    sums_in,
    own_sum,
    latents,
    windows,
    first_weight,
    first_back,
    field,
    second,
    slope_first,
    back_field,
    back_first,
    weights,
    sibling_out,
    sibling_in,
    pooled_all,
    grads,
    head_in,
    sib_sems,
    parts_send,
    parts_recv,
    sums_sems,
    halo_send,
    halo_recv,
    w_send,
    w_recv,
    s_recv,
    pool_sems,
    far_send,
    far_recv,
    near_sems,
    head_sems,
    in_sems,
):
    dp = lax.axis_index("dp")
    mp = lax.axis_index("mp")
    core = lax.rem(dp, 2)
    x = lax.rem(dp // 2, 4)
    y_hi = dp // 8
    y_lo = lax.rem(mp, 2)
    right_x, left_x, far_x = lax.rem(x + 1, 4), lax.rem(x + 3, 4), lax.rem(x + 2, 4)
    sibling = dp + 1 - 2 * core
    right = y_hi * 8 + right_x * 2 + core
    left = y_hi * 8 + left_x * 2 + core
    other_dp = (1 - y_hi) * 8 + x * 2 + core
    other_mp = mp + 1 - 2 * y_lo
    mine, beside = y_hi * 4, (1 - y_hi) * 4
    z = mp // 2
    block_row, block_column = mp // 8, lax.rem(mp, 8)

    def near(dz, dy):
        return lax.rem(z + dz + 16, 16) * 2 + y_lo + dy * (1 - 2 * y_lo)

    def far(dk):
        return lax.rem(mp + 8 * dk, NMP)

    def send(src, dst, send_sem, recv_sem, to_dp, to_mp):
        pltpu.make_async_remote_copy(
            src_ref=src,
            dst_ref=dst,
            send_sem=send_sem,
            recv_sem=recv_sem,
            device_id=(to_dp, to_mp),
            device_id_type=pl.DeviceIdType.MESH,
        ).start()

    def wait(ref, sem):
        pltpu.make_async_copy(ref, ref, sem).wait()

    barrier = pltpu.get_barrier_semaphore()

    def greet(to_dp, to_mp):
        pl.semaphore_signal(
            barrier, inc=1, device_id=(to_dp, to_mp), device_id_type=pl.DeviceIdType.MESH
        )

    @pl.loop(1, NMP)
    def _(d):
        greet(dp, lax.rem(mp + d, NMP))

    @pl.loop(1, NDP)
    def _(d):
        greet(lax.rem(dp + d, NDP), mp)

    greet(other_dp, other_mp)

    loads = [
        pltpu.make_async_copy(far, near, in_sems.at[n])
        for n, (far, near) in enumerate(
            (
                (cmid_far, cmid_ref),
                (mod_far, mod_ref),
                (hidden_far, hidden_ref),
                (head_far, head_ref),
                (cin_far, cin_ref),
                (patch_far, patch_ref),
                (text_far, text_ref),
            )
        )
    ]
    for load in loads:
        load.start()

    loads[0].wait()

    @pl.loop(0, 18)
    def _(t):
        own = cmid_ref[t + 9].astype(F32)
        sibling_out[t] = jnp.concatenate([own, jnp.zeros((8, CH), F32)], axis=0).astype(BF16)

    pl.semaphore_wait(barrier, NMP - 1 + NDP - 1 + 1)

    send(sibling_out, sibling_in, sib_sems.at[0], sib_sems.at[1], sibling, mp)

    for load in loads[1:4]:
        load.wait()

    modulation = mod_ref[step_ref[0]].astype(F32)
    across = lax.broadcasted_iota(jnp.int32, (FEAT, FEAT), 1)
    diagonal = lax.broadcasted_iota(jnp.int32, (FEAT, FEAT), 0) == across
    shift, gain = (
        jnp.sum(jnp.where(diagonal, modulation[n : n + 1], 0.0), axis=1, keepdims=True)
        for n in range(2)
    )
    gain = 1.0 + gain

    @pl.loop(0, 4)
    def _(n):
        halves = []
        for f in range(2):
            columns = pl.ds(pl.multiple_of(n * 256 + f * 1024, 256), 256)
            block = (hidden_ref[:, columns].astype(F32) * gain + shift).astype(BF16)
            modulated[:, columns] = block
            halves.append(dot(head_ref[...], block))
        total = jnp.concatenate(halves, axis=0).T
        parts_out[n] = total.astype(BF16).reshape(8, Q, 128)

    for dk in (2, 1, 3, 0):
        for n, (dz, dy) in enumerate(NEAR):
            to = near(dz, dy)
            block = parts_out.at[lax.rem(to // 8 + dk, 4), lax.rem(to, 8)]
            send(block, parts_in.at[dk, n], parts_send, parts_recv.at[dk], dp, to)

    wait(sibling_in, sib_sems.at[1])

    def shard_rows(j):
        return pl.ds(pl.multiple_of(SHARD * j, 16), SHARD)

    own_rows = shard_rows(dp // 2)

    @pl.loop(0, 18)
    def _(t):
        own = sibling_out[t].astype(F32)
        other = sibling_in[t].astype(F32)
        low = jnp.where(core == 0, own, other)
        high = jnp.where(core == 0, other, own)
        weights[t, own_rows, :] = jnp.concatenate([low[0:24], high[0:24]], axis=0).astype(BF16)

    z_odd = lax.rem(z, 2)
    solo = 1 + lax.rem(y_lo + z, 2)
    lent = 3 - solo
    SOLO, LENT = 1, 2
    index = (0, solo, lent)

    def piece(slot, j, c):
        return weights.at[pl.ds(3 * (2 * index[slot] + c), 3), shard_rows(j), :]

    def part(slot, j, t):
        return weights.at[3 * (2 * index[slot] + core) + t, shard_rows(j), :]

    def pass_on(slot, j, kind, to_dp, to_mp, to_slot=None):
        to_slot = slot if to_slot is None else to_slot
        for t in range(3):
            block = part(slot, j, t)
            send(block, block, w_send, w_recv.at[kind, to_slot, t], to_dp, to_mp)

    def relay(slot, j, kind, *onward):
        if slot == SOLO and kind in (LEFT, RIGHT, FAR2):
            onward += ((kind, LENT, dp, mp + 1 - 2 * y_lo),)
        elif slot == SOLO:
            onward += ((kind, LENT, dp, mp + 2 - 4 * z_odd),)
        if slot == 0 and kind in (LEFT, RIGHT, FAR):
            onward += (({LEFT: LEFT2, RIGHT: RIGHT2, FAR: FAR2}[kind], 0, other_dp, other_mp),)
        for t in range(3):
            block = part(slot, j, t)
            wait(block, w_recv.at[kind, slot, t])
            for to_kind, to_slot, to_dp, to_mp, *only in onward:
                if only and t not in only[0]:
                    continue
                send(block, block, w_send, w_recv.at[to_kind, to_slot, t], to_dp, to_mp)
            send(block, block, w_send, s_recv.at[kind, slot], sibling, mp)

    BESIDE, LEFT, RIGHT, LEFT2, RIGHT2, FAR, FAR2 = range(7)
    own = mine + x
    kinds = (
        (BESIDE, beside + x),
        (LEFT, mine + left_x),
        (RIGHT, mine + right_x),
        (LEFT2, beside + left_x),
        (RIGHT2, beside + right_x),
        (FAR, mine + far_x),
        (FAR2, beside + far_x),
    )
    pass_on(LENT, own, BESIDE, other_dp, other_mp, SOLO)
    pass_on(0, own, LEFT, right, mp)
    pass_on(0, own, RIGHT, left, mp)
    pass_on(SOLO, own, LEFT, right, mp)
    pass_on(SOLO, own, RIGHT, left, mp)

    for load in loads[4:7]:
        load.wait()

    first_weight[...] = jnp.zeros_like(first_weight)
    for a in range(2):
        for b in range(3):
            for c in range(3):
                tap = cin_ref[9 + 9 * a + 3 * b + c]
                for j in range(2):
                    at = b * 128 + a * 64 + (c + j) * 16
                    first_weight[at : at + 16, j * CH : (j + 1) * CH] = tap
                at = (a * 3 + b) * 16
                first_back[at : at + 16, c * CH : (c + 1) * CH] = tap

    for f in range(2):
        head_wide[f] = jnp.zeros((FEAT, 128), BF16)
        head_wide[f, :, f * 64 : (f + 1) * 64] = head_ref[...].astype(F32).T.astype(BF16)
    place[...] = window_placement()

    def near_sum(dk):
        wait(parts_in.at[dk], parts_recv.at[dk])
        total = parts_out[lax.rem(block_row + dk, 4), block_column].astype(F32)
        for n in range(len(NEAR)):
            total = total + parts_in[dk, n].astype(F32)
        return total

    for dk in (2, 1, 3):
        sums_out[dk - 1] = near_sum(dk).astype(BF16)
        send(sums_out.at[dk - 1], sums_in.at[dk - 1], sums_sems.at[0], sums_sems.at[1], dp, far(dk))
    own_sum[...] = near_sum(0)

    relay(SOLO, beside + x, BESIDE, (LEFT2, SOLO, right, mp), (RIGHT2, SOLO, left, mp))
    relay(0, mine + left_x, LEFT, (FAR, 0, right, mp, (0, 1)))
    relay(0, mine + right_x, RIGHT, (FAR, 0, left, mp, (2,)))
    relay(SOLO, mine + left_x, LEFT, (FAR, SOLO, right, mp))
    relay(SOLO, mine + right_x, RIGHT)
    pass_on(0, own, BESIDE, other_dp, other_mp)

    relay(SOLO, beside + right_x, RIGHT2, (FAR2, SOLO, left, mp))
    relay(SOLO, beside + left_x, LEFT2)

    wait(sums_in, sums_sems.at[1])
    latent = own_sum[...]
    for n in range(3):
        latent = latent + sums_in[n].astype(F32)
    latents[2] = latent.astype(BF16)
    for n, d in enumerate((-2, -1, 1, 2)):
        to = lax.rem(mp + d + NMP, NMP)
        send(latents.at[2], latents.at[2 - d], halo_send.at[n], halo_recv.at[n], dp, to)

    relay(SOLO, mine + far_x, FAR)
    relay(0, mine + far_x, FAR)
    relay(SOLO, beside + far_x, FAR2)
    relay(0, beside + x, BESIDE)
    relay(LENT, beside + x, BESIDE)

    for n, d in enumerate((-2, -1, 1, 2)):
        wait(latents.at[2 - d], halo_recv.at[n])

    pair = lax.broadcasted_iota(jnp.int32, (5 * Q, 1), 0) // Q + mp - 2
    tokens = jnp.where((pair >= 0) & (pair < NMP), latents[...].reshape(5 * Q, 128).astype(F32), 0.0)
    around = jnp.concatenate([from_previous(tokens), tokens, from_next(tokens)], axis=1)
    placed = dot(around.astype(BF16), place[...]).astype(BF16)
    for p in range(5):
        for row in range(2):
            rows = slice(p * Q, (p + 1) * Q)
            windows[1, 2 * p + row] = placed[rows, row * 128 : (row + 1) * 128]
            windows[0, 2 * p + row] = placed[rows, 256 + row * 128 : 256 + (row + 1) * 128]
    for f in range(2):
        taps = jnp.concatenate([windows[f, b : b + 8].reshape(8 * Q, 128) for b in range(3)], axis=1)
        inside = rows_inside(8 * Q, 2 * mp - 3)
        columns = []
        for j in range(2):
            value = dot(taps, first_weight[:, j * CH : (j + 1) * CH])
            gate = sigmoid(value)
            columns.append(value * gate * inside)
            slope = gate * (1.0 + value * (1.0 - gate))
            slope_first[f, :, j * Q : (j + 1) * Q, :] = slope[2 * Q : 6 * Q].reshape(4, Q, CH)
        spread(field, f, columns[0], columns[1], False)

    for kind, j in kinds[1:]:
        if kind in (LEFT2, RIGHT2, FAR2):
            relay(0, j, kind)
        relay(LENT, j, kind)
    for slot in range(3):
        for kind, j in kinds:
            wait(piece(slot, j, 1 - core), s_recv.at[kind, slot])

    def tap(a, b):
        at = 9 * a + 3 * b
        return weights[at : at + 3].reshape(3 * CH, CH)

    def middle(starts):
        early, late = None, None
        for b in range(3):
            both = jnp.concatenate([tap(1, b), tap(0, b)], axis=1)
            sources = [
                jnp.concatenate([field[f, r + b : r + b + 2].reshape(128, 3 * CH) for r in starts], axis=0)
                for f in range(2)
            ]
            terms = dot(sources[0], both), dot(sources[1], tap(1, b))
            early = terms[0] if early is None else early + terms[0]
            late = terms[1] if late is None else late + terms[1]
        late = late + early[:, CH : 2 * CH]
        for n, r in enumerate(starts):
            second[0, r * 64 : r * 64 + 128] = early[n * 128 : (n + 1) * 128, 0:CH]
            second[1, r * 64 : r * 64 + 128] = late[n * 128 : (n + 1) * 128]

    middle((2,))

    for f in range(2):
        value = second[f, 128:256]
        decoded = (value * sigmoid(value)).astype(BF16).astype(F32)
        pooled_all[mp, :, f * CH : (f + 1) * CH] = jnp.sum(decoded, axis=0, keepdims=True)

    @pl.loop(1, NMP)
    def _(d):
        to = lax.rem(mp + d, NMP)
        send(pooled_all.at[mp], pooled_all.at[mp], pool_sems.at[0], pool_sems.at[1], dp, to)

    middle((0, 4))
    row = lax.broadcasted_iota(jnp.int32, (6 * 64, 1), 0) // 64 + 2 * mp - 2
    inside = jnp.where((row >= 0) & (row < 2 * NMP), 1.0, 0.0)
    for f in range(2):
        value = second[f]
        gate = sigmoid(value)
        second[f] = gate * (1.0 + value * (1.0 - gate)) * inside

    wait(pooled_all.at[pl.ds(0, NMP - 1)], pool_sems.at[1])

    sums = pooled_all[0]
    for s in range(1, NMP):
        sums = sums + pooled_all[s]
    sums = sums * (1.0 / CELLS)
    pooled = jnp.concatenate([sums[:, 0:CH], sums[:, CH : 2 * CH]], axis=0)
    rows = dot(three_parts(pooled), patch_ref[...])
    embedded = rows[0:2] + rows[2:4] + rows[4:6]
    text = text_ref[...]
    embed_square = jnp.sum(embedded * embedded, axis=1, keepdims=True) + 1e-6
    embed_scale = lax.rsqrt(embed_square)
    text_scale = lax.rsqrt(jnp.sum(text * text, axis=1, keepdims=True) + 1e-6)
    cosine = jnp.sum(embedded * text, axis=1, keepdims=True) * embed_scale * text_scale
    reward_ref[...] = jnp.broadcast_to(50.0 * (cosine[0:1] + cosine[1:2]), (1, 128))
    embed_grad = 50.0 * embed_scale * (text * text_scale - embedded * (cosine * embed_scale))
    rows = dot(three_parts(embed_grad), patch_ref[...], NT)
    pool_grad = (rows[0:2] + rows[2:4] + rows[4:6]) * (1.0 / CELLS)

    for f in range(2):
        grad = (second[f] * pool_grad[f : f + 1]).reshape(6, 64, CH)
        spread(back_field, f, grad[:, 0:Q].reshape(6 * Q, CH), grad[:, Q:].reshape(6 * Q, CH), True)
    row = lax.broadcasted_iota(jnp.int32, (4 * 64, 1), 0) // 64 + 2 * mp - 1
    inside = jnp.where((row >= 0) & (row < 2 * NMP), 1.0, 0.0)
    late, early = None, None
    for b in range(3):
        sources = [back_field[f, 2 - b : 6 - b].reshape(4 * 64, 3 * CH) for f in range(2)]
        both = [
            jnp.concatenate([weights[9 * a + 3 * b + c] for c in range(3)], axis=1) for a in range(2)
        ]
        terms = dot(sources[1], jnp.concatenate([both[1], both[0]], axis=0), NT), dot(sources[0], both[1], NT)
        late = terms[0] if late is None else late + terms[0]
        early = terms[1] if early is None else early + terms[1]
    grad_field = (early + late[:, CH : 2 * CH], late[:, 0:CH])
    for f in range(2):
        total = grad_field[f]
        total = total * slope_first[f].reshape(4 * 64, CH) * inside
        total = total.reshape(4, 64, CH)
        spread(back_first, f, total[:, 0:Q].reshape(4 * Q, CH), total[:, Q:].reshape(4 * Q, CH), True)

    taps = [dot(back_first[f].reshape(4 * 64, 3 * CH), first_back[...], NT) for f in range(2)]
    blocks = []
    for f in range(2):
        for i in range(2):
            for j in range(2):
                total = None
                for a in range(2):
                    if f + 1 - a > 1:
                        continue
                    for b in range(3):
                        at = (i + 2 - b) * 64 + j * Q
                        lane = (a * 3 + b) * 16
                        term = taps[f + 1 - a][at : at + Q, lane : lane + 16]
                        total = term if total is None else total + term
                blocks.append(total)
    grads[block_row, block_column] = jnp.concatenate(blocks, axis=1).astype(BF16)

    def spread_near(row):
        block = grads.at[row, block_column]
        for dz, dy in NEAR:
            send(block, block, near_sems.at[0], near_sems.at[1], dp, near(dz, dy))

    for dk in (2, 1, 3):
        block = grads.at[block_row, block_column]
        send(block, block, far_send, far_recv.at[dk - 1], dp, far(dk))
    spread_near(block_row)
    for dk in (1, 3, 2):
        row = lax.rem(block_row + 4 - dk, 4)
        wait(grads.at[row, block_column], far_recv.at[dk - 1])
        spread_near(row)
    wait(grads.at[:, pl.ds(0, 7)], near_sems.at[1])
    token_grad = grads[...].reshape(NMP * Q, 128)

    early = dot(modulated[:, 0:1024], token_grad).T
    late = dot(modulated[:, 1024:2048], token_grad).T
    part = early[0:64] + late[64:128]
    rest = [part[r * 16 : (r + 1) * 16, 128:FEAT] for r in range(4)]
    head_in[dp, 0:64, :] = part[:, 0:128].astype(BF16)
    head_in[dp, 64:80, :] = jnp.concatenate(rest, axis=1).astype(BF16)

    @pl.loop(1, NDP)
    def _(d):
        block = head_in.at[dp]
        send(block, block, head_sems.at[0], head_sems.at[1], lax.rem(dp + d, NDP), mp)

    def hidden_part(f):
        value = dot(head_wide[f], grads[...].reshape(NMP * Q, 128), NT) * gain
        hidden_grad_ref[:, f * 1024 : (f + 1) * 1024] = value.astype(BF16)

    hidden_part(0)
    hidden_part(1)

    wait(head_in.at[pl.ds(0, NDP - 1)], head_sems.at[1])
    total = head_in[0].astype(F32)
    for s in range(1, NDP):
        total = total + head_in[s].astype(F32)
    head_grad_ref[:, 0:128] = total[0:64]
    for r in range(4):
        head_grad_ref[r * 16 : (r + 1) * 16, 128:FEAT] = total[64:80, r * 32 : (r + 1) * 32]

    wait(head_in.at[pl.ds(0, NDP - 1)], head_sems.at[0])
    wait(sibling_out, sib_sems.at[0])
    wait(parts_in, parts_send)
    for n in range(4):
        wait(latents.at[2], halo_send.at[n])
    wait(weights.at[:, pl.ds(0, 7 * SHARD), :], w_send)
    wait(pooled_all.at[pl.ds(0, NMP - 1)], pool_sems.at[0])
    wait(sums_in, sums_sems.at[0])
    wait(grads.at[0, pl.ds(0, 3)], far_send)
    wait(grads.at[:, pl.ds(0, 7)], near_sems.at[0])


def body(hidden, mod_table, timestep, head_weight, conv_in, conv_mid, patch_weight, text_emb):
    vmem = pl.BlockSpec(memory_space=pltpu.VMEM)
    dma = pltpu.SemaphoreType.DMA
    reward, head_grad, hidden_grad = pl.pallas_call(
        kernel,
        out_shape=(
            pltpu.VMEM((1, 128), F32),
            pltpu.VMEM((64, FEAT), F32),
            pltpu.VMEM((FEAT, 2048), BF16),
        ),
        in_specs=[pl.BlockSpec(memory_space=pltpu.SMEM)] + [pl.BlockSpec(memory_space=pltpu.HBM)] * 7,
        out_specs=(vmem, vmem, vmem),
        scratch_shapes=[
            pltpu.VMEM((FEAT, 2048), BF16),
            pltpu.VMEM((50, 2, FEAT), BF16),
            pltpu.VMEM((64, FEAT), BF16),
            pltpu.VMEM((27, 24, CH), BF16),
            pltpu.VMEM((27, C, CH), BF16),
            pltpu.VMEM((CH, EMB), BF16),
            pltpu.VMEM((1, EMB), F32),
            pltpu.VMEM((FEAT, 2048), BF16),
            pltpu.VMEM((2, FEAT, 128), BF16),
            pltpu.VMEM((384, 512), BF16),
            pltpu.VMEM((4, 8, Q, 128), BF16),
            pltpu.VMEM((4, 7, Q, 128), BF16),
            pltpu.VMEM((3, Q, 128), BF16),
            pltpu.VMEM((3, Q, 128), BF16),
            pltpu.VMEM((Q, 128), F32),
            pltpu.VMEM((5, Q, 128), BF16),
            pltpu.VMEM((2, 10, Q, 128), BF16),
            pltpu.VMEM((384, 2 * CH), BF16),
            pltpu.VMEM((96, 3 * CH), BF16),
            pltpu.VMEM((2, 8, 64, 3 * CH), BF16),
            pltpu.VMEM((2, 6 * 64, CH), F32),
            pltpu.VMEM((2, 4, 64, CH), F32),
            pltpu.VMEM((2, 6, 64, 3 * CH), BF16),
            pltpu.VMEM((2, 4, 64, 3 * CH), BF16),
            pltpu.VMEM((18, CH, CH), BF16),
            pltpu.VMEM((18, 32, CH), BF16),
            pltpu.VMEM((18, 32, CH), BF16),
            pltpu.VMEM((NMP, 1, 2 * CH), F32),
            pltpu.VMEM((4, 8, Q, 128), BF16),
            pltpu.VMEM((NDP, 80, 128), BF16),
            dma((2,)),
            dma,
            dma((4,)),
            dma((2,)),
            dma((4,)),
            dma((4,)),
            dma,
            dma((7, 3, 3)),
            dma((7, 3)),
            dma((2,)),
            dma,
            dma((3,)),
            dma((2,)),
            dma((2,)),
            dma((7,)),
        ],
        compiler_params=pltpu.CompilerParams(
            collective_id=0, has_side_effects=True, vmem_limit_bytes=48 * 1024 * 1024
        ),
        name="guided_step",
    )(
        timestep,
        *(
            pltpu.with_memory_space_constraint(operand, pltpu.HBM)
            for operand in (
                hidden.T,
                mod_table,
                head_weight.T,
                jnp.transpose(conv_mid, (1, 0, 2)),
                jnp.transpose(conv_in, (1, 0, 2)),
                patch_weight,
                text_emb,
            )
        ),
    )
    return (reward[0, 0:1], head_grad.T, hidden_grad.T)


def solution(mesh):
    in_specs = (
        P("dp", "mp"),
        P(None, None, "mp"),
        P("dp"),
        P("mp", None),
        P(),
        P("dp", None, None),
        P(),
        P("dp", None),
    )
    out_specs = (P("dp"), P("mp", None), P("dp", "mp"))
    return jax.shard_map(body, mesh=mesh, in_specs=in_specs, out_specs=out_specs, check_vma=False)
```
